128 devices in a mesh: grp: 4 (over x_hi, core), chol: 32 (over y, x_lo, z).
Axes of the slice: x: 4 (x_hi: 2, x_lo: 2; x = x_hi * 2 + x_lo), y: 4, z: 4, core: 2. Of those that a mesh axis runs over, the one named last changes fastest.
Arguments:
- green: bfloat16 [1024, 2, 16, 128], P('chol', None, 'grp'), may hold values from -0.23925781 to 0.23925781
- chol_blocks: bfloat16 [8192, 128, 128], P(('grp', 'chol')), may hold values from -0.119628906 to 0.119628906
- block_ids: int32 [8192, 2], P(('grp', 'chol')), may hold values from 0 to 15, all different within a row
- noise: float32 [16, 8192], P(None, ('grp', 'chol')), may hold values from -6 to 6
- weights: float32 [16], P('grp'), may hold values from 0.5 to 2
- copies: int32 [16], P('grp'), may hold values from 0 to 4, as said below
- owners: int32 [16, 4], P('grp'), may hold values from 0 to 3, as said below
Outputs:
- force_bias: float32 [2, 16, 8192], P(None, None, ('grp', 'chol'))
- energy: float32 [2, 16], P(None, 'grp')
- new_weights: float32 [16], P('grp')
- moved_green: bfloat16 [1024, 2, 16, 128], P('chol', None, 'grp')
- moved_weights: float32 [16], P('grp')
The draws below stay inside these ranges and needn't reach their ends.
Inputs may be any that keep to these rules, and one draw needn't show every extreme that they name: The copies of all walkers sum to 16; some walker has 4 copies and some have none. `owners`: over the live entries (j < copies[w]) every task group is named exactly 4 times; entries with j >= copies[w] are ignored. `block_ids`: each vector names 2 different orbital blocks.
All inputs are finite; a program needn't handle non-finite values.
Results may differ from the reference program's by a relative error of at most 0.011.
The reference program's roundings to bfloat16 on the way count: a program that leaves them out, or rounds other values in their place, can miss the bound.
Values may be sent and summed in bfloat16 or wider, within the bound.
A program may use at most 64 MiB of HBM per device.

```python
import math
import jax
import jax.numpy as jnp
from jax import lax

M = 1024
NEL = 128
NCHOL = 8192
BLOCK = 64
NBV = 2
KMAX = 4
WG = 4
WALKERS = 16


def branching(key):
    base = jax.random.fold_in(key, 11)
    key_pick, key_order, key_owner, key_spare = jax.random.split(base, 4)
    families = WALKERS // KMAX
    parents = jax.random.randint(key_pick, (families, KMAX), 0, KMAX)
    parents = parents.at[0].set(0)
    tally = jnp.sum((parents[:, :, None] == jnp.arange(KMAX)[None, None, :]).astype(jnp.int32), axis=1)
    order = jax.random.permutation(key_order, WALKERS)
    counts = jnp.zeros((WALKERS,), jnp.int32).at[order].set(tally.reshape(-1))
    labels = jax.random.permutation(key_owner, jnp.arange(WALKERS, dtype=jnp.int32) // WG)
    starts = jnp.cumsum(counts) - counts
    index = jnp.clip(starts[:, None] + jnp.arange(KMAX)[None, :], 0, WALKERS - 1)
    filled = labels[index]
    spare = jax.random.randint(key_spare, (WALKERS, KMAX), 0, WALKERS // WG)
    chosen = jnp.where(jnp.arange(KMAX)[None, :] < counts[:, None], filled, spare)
    return (counts.astype(jnp.int32), chosen.astype(jnp.int32))


def draw_copies(key, part):
    return branching(key)[0]


def draw_owners(key, part):
    return branching(key)[1]


def steps_of(stream_key, extent, pieces, smallest, high):
    def one(position, parts):
        draws = jax.random.uniform(jax.random.fold_in(jax.random.fold_in(stream_key, 6), position), (parts,), jnp.float32, smallest / len(pieces), high / len(pieces))
        return jnp.repeat(jnp.exp(draws), extent[position] // parts).reshape((-1,) + (1,) * (len(extent) - position - 1))

    level = one(*pieces[0])
    for cut in pieces[1:]:
        level = level * one(*cut)
    return level


def picks_of(own_key, rows, amount, top, lift):
    sequence = jax.random.permutation(jax.random.fold_in(own_key, 1), amount)
    boost = sequence
    for power in range(3):
        boost = boost * boost // amount
    boost = boost * lift // amount
    lots = jax.random.randint(jax.random.fold_in(own_key, 2), (rows, amount), 0, 4096) + boost
    sure = jax.random.permutation(jax.random.fold_in(own_key, 3), rows)[jnp.arange(amount) % rows]
    lots = jnp.where(jnp.arange(rows)[:, None] == sure[None, :], 1 << 14, lots)
    merit = lots * amount + jnp.arange(amount)
    return lax.top_k(merit.astype(jnp.int32), top)[1].astype(jnp.int32)


def centred(key, shape, scale, reach, shards=(), kind=jnp.bfloat16):
    gain = steps_of(key, shape, shards, -0.22, 0.18) if shards else 1.0
    result = jax.random.normal(key, shape, jnp.float32) * scale * gain
    return jnp.minimum(jnp.maximum(result, -reach), reach).astype(kind)


def setup_inputs(seed: int = 0) -> dict:
    splits = jax.random.split(jax.random.key(seed), 8)
    return {
        "green": centred(splits[0], (M, 2, WALKERS, NEL), 0.04, 0.23925781, ((0, 32), (2, 4))),
        "chol_blocks": centred(splits[1], (NCHOL, NEL, NBV * BLOCK), 0.02, 0.119628906, ((0, 128),)),
        "block_ids": picks_of(splits[2], NCHOL, M // BLOCK, NBV, 0),
        "noise": centred(splits[3], (WALKERS, NCHOL), 1.0, 6.0, ((1, 128),), jnp.float32),
        "weights": jnp.clip(jnp.exp(math.log(2.0) - 1.3862944 * jax.random.uniform(splits[4], (WALKERS,), jnp.float32) ** steps_of(splits[4], (WALKERS,), ((0, 4),), -0.2, 0.2)), 0.5, 2.0),
        "copies": draw_copies(jax.random.fold_in(splits[7], 71), 0),
        "owners": draw_owners(jax.random.fold_in(splits[7], 71), 0),
    }


time_step = 0.005

def column_table(block_ids):
    offsets = jnp.arange(BLOCK, dtype=jnp.int32)
    table = block_ids.astype(jnp.int32)[:, :, None] * BLOCK + offsets[None, None, :]
    return table.reshape(block_ids.shape[0], block_ids.shape[1] * BLOCK)

def largest_divisor(total, limit):
    best = 1
    for candidate in range(1, total + 1):
        if total % candidate == 0 and candidate <= limit:
            best = candidate
    return best

def reference(green, chol_blocks, block_ids, noise, weights, copies, owners):
    orbitals, pairs, walkers, electrons = green.shape
    flat = green.reshape(orbitals, pairs * walkers * electrons)
    columns = column_table(block_ids)
    vector_count, width = columns.shape
    size = largest_divisor(vector_count, 16)
    count = vector_count // size
    identity = jnp.eye(electrons, dtype=jnp.float32)
    highest = lax.Precision.HIGHEST
    root = math.sqrt(time_step)

    def one_block(items):
        part_blocks, part_columns, part_fields = items
        selected = jnp.take(flat, part_columns, axis=0).astype(jnp.float32)
        product = jnp.einsum('vik,vkx->vix', part_blocks.astype(jnp.float32), selected, precision=highest)
        product = lax.optimization_barrier(product.astype(jnp.bfloat16)).astype(jnp.float32)
        product = product.reshape(size, electrons, pairs, walkers, electrons)
        traces = 2.0 * jnp.einsum('vicwj,ij->cwv', product, identity, precision=highest)
        real_part = product[:, :, 0]
        imag_part = product[:, :, 1]
        real_real = jnp.einsum('viwj,vjwi->wv', real_part, real_part, precision=highest)
        imag_imag = jnp.einsum('viwj,vjwi->wv', imag_part, imag_part, precision=highest)
        real_imag = jnp.einsum('viwj,vjwi->wv', real_part, imag_part, precision=highest)
        bias_real = traces[0]
        bias_imag = traces[1]
        energy_real = 0.5 * (bias_real * bias_real - bias_imag * bias_imag) - (real_real - imag_imag)
        energy_imag = bias_real * bias_imag - 2.0 * real_imag
        shift_real = -root * bias_real
        shift_imag = -root * bias_imag
        phase_real = part_fields * shift_real - 0.5 * (shift_real * shift_real - shift_imag * shift_imag)
        phase_imag = part_fields * shift_imag - shift_real * shift_imag
        energy = jnp.stack([lax.optimization_barrier(jnp.sum(energy_real, axis=1)), lax.optimization_barrier(jnp.sum(energy_imag, axis=1))])
        phase = jnp.stack([lax.optimization_barrier(jnp.sum(phase_real, axis=1)), lax.optimization_barrier(jnp.sum(phase_imag, axis=1))])
        return (traces, energy, phase)
    blocks_in = chol_blocks.reshape(count, size, electrons, width)
    columns_in = columns.reshape(count, size, width)
    fields_in = jnp.moveaxis(noise.reshape(walkers, count, size), 1, 0)
    traces, energies, phases = lax.map(one_block, (blocks_in, columns_in, fields_in))
    force_bias = jnp.moveaxis(traces, 0, 2).reshape(2, walkers, vector_count)
    energy = lax.optimization_barrier(jnp.sum(energies, axis=0))
    phase = lax.optimization_barrier(jnp.sum(phases, axis=0))
    new_weights = weights * jnp.exp(phase[0]) * jnp.maximum(jnp.cos(phase[1]), 0.0)
    groups = walkers // WG
    kept = jnp.arange(KMAX, dtype=jnp.int32)[None, :] < copies[:, None]
    targets = jnp.arange(groups, dtype=jnp.int32)
    hits = ((owners[:, :, None] == targets[None, None, :]) & kept[:, :, None]).astype(jnp.int32)
    hits = hits.reshape(walkers * KMAX, groups)
    ranks = jnp.cumsum(hits, axis=0, dtype=jnp.int32) - hits
    slots = lax.optimization_barrier(jnp.sum(hits * (ranks + targets[None, :] * WG), axis=1, dtype=jnp.int32))
    live = lax.optimization_barrier(jnp.sum(hits, axis=1, dtype=jnp.int32)) > 0
    positions = jnp.arange(walkers, dtype=jnp.int32)
    route = ((slots[:, None] == positions[None, :]) & live[:, None]).astype(jnp.float32)
    route = lax.optimization_barrier(jnp.sum(route.reshape(walkers, KMAX, walkers), axis=1))
    moved_green = jnp.einsum('mcwn,ws->mcsn', green.astype(jnp.float32), route, precision=highest).astype(jnp.bfloat16)
    moved_weights = lax.optimization_barrier(jnp.sum(route * new_weights[:, None], axis=0))
    return (force_bias, energy, new_weights, moved_green, moved_weights)
```

```python
import functools
import math

import jax
import jax.numpy as jnp
from jax import lax
from jax.experimental import pallas as pl
from jax.experimental.pallas import tpu as pltpu
from jax.sharding import PartitionSpec as P

MESH = pl.DeviceIdType.MESH
BF16 = jnp.bfloat16
F32 = jnp.float32
KMAX = 4
GROUPS = 4
WG = 4
ROOT = math.sqrt(0.005)
MB = 2**20

STREAMS = (
    (0, 0, 2, "xyz"),
    (1, 0, 2, "yzx"),
    (2, 0, 2, "zxy"),
    (3, 0, 1, "xyz"),
    (3, 1, 1, "yzx"),
)


def position():
    grp = lax.axis_index("grp")
    chol = lax.axis_index("chol")
    x = (grp // 2) * 2 + (chol // 4) % 2
    return x, chol // 8, chol % 4, grp % 2


def device(x, y, z, core):
    return ((x // 2) * 2 + core, y * 8 + (x % 2) * 4 + z)


def gather_kernel(
    shard, vectors, ids, noise, meta, green,
    gathered, vectors2, ids2, noise2, meta_all, green_all,
    local_sem, send_sem, recv_sem, pair_send, pair_recv, group_send, group_recv,
):
    x, y, z, core = position()
    grp = lax.axis_index("grp")
    here = {"x": x, "y": y, "z": z}
    sibling = device(x, y, z, 1 - core)
    across = [device((x + 2) % 4, y, z, core), device((x + 2) % 4, y, z, 1 - core)]
    neighbours = []
    for axis in "xyz":
        for step in (1, 3):
            there = dict(here)
            there[axis] = (here[axis] + step) % 4
            neighbours.append(device(there["x"], there["y"], there["z"], core))
    barrier = pltpu.get_barrier_semaphore()
    everyone = neighbours + [sibling] + across
    for target in everyone:
        pl.semaphore_signal(barrier, inc=1, device_id=target, device_id_type=MESH)

    local = [
        pltpu.make_async_copy(shard, gathered.at[:, x, y, z], local_sem.at[0]),
        pltpu.make_async_copy(meta, meta_all.at[grp], local_sem.at[1]),
        pltpu.make_async_copy(green, green_all.at[grp], local_sem.at[2]),
    ]
    for copy in local:
        copy.start()
    pl.semaphore_wait(barrier, len(everyone))

    def remote(source, target, send, recv, where):
        return pltpu.make_async_remote_copy(
            src_ref=source, dst_ref=target, send_sem=send, recv_sem=recv,
            device_id=where, device_id_type=MESH,
        )

    others = [
        remote(ids, ids2, pair_send.at[0], pair_recv.at[0], sibling),
        remote(noise, noise2, pair_send.at[1], pair_recv.at[1], sibling),
        remote(vectors, vectors2, pair_send.at[2], pair_recv.at[2], sibling),
    ]
    for i, target in enumerate([sibling] + across):
        others.append(remote(meta, meta_all.at[grp], group_send.at[0, i], group_recv.at[0, i], target))
        others.append(remote(green, green_all.at[grp], group_send.at[1, i], group_recv.at[1, i], target))

    def view(stream, free, at, rows):
        walker, first, count, _ = STREAMS[stream]
        index = [slice(None) if axis in free else at[axis] for axis in "xyz"]
        return gathered.at[
            (walker, *index, pl.ds(rows[0], rows[1]), pl.ds(first * 128, count * 128))
        ]

    local[0].wait()
    pending = [[] for _ in STREAMS]
    for phase in range(3):
        moves = []
        for stream, (_, _, _, order) in enumerate(STREAMS):
            for copy in pending[stream]:
                copy.wait()
            axis, free = order[phase], order[:phase]
            up, down = dict(here), dict(here)
            up[axis] = (here[axis] + 1) % 4
            down[axis] = (here[axis] + 3) % 4
            to_up = device(up["x"], up["y"], up["z"], core)
            to_down = device(down["x"], down["y"], down["z"], core)

            def make(kind, at, rows, target):
                part = view(stream, free, at, rows)
                return remote(
                    part, part, send_sem.at[stream, phase, kind], recv_sem.at[stream, phase, kind], target
                )

            first = [make(0, here, (0, 32), to_up), make(1, here, (0, 32), to_down)]
            second = [make(2, down, (0, 16), to_up), make(3, up, (16, 16), to_down)]
            for copy in first:
                copy.start()
            moves.append((first, second))
        if phase == 0:
            for copy in others:
                copy.start()
        for first, second in moves:
            for one, two in zip(first, second):
                one.wait_recv()
                two.start()
        for stream, (first, second) in enumerate(moves):
            for copy in first:
                copy.wait_send()
            pending[stream] = second
    for copies in pending:
        for copy in copies:
            copy.wait()
    for copy in others:
        copy.wait()
    for copy in local[1:]:
        copy.wait()


def gather(shard, vectors, ids, noise, meta, green):
    spec = pl.BlockSpec(memory_space=pl.ANY)
    streams = len(STREAMS)
    shape = jax.ShapeDtypeStruct
    return pl.pallas_call(
        gather_kernel,
        out_shape=(
            shape((WG, 4, 4, 4) + shard.shape[1:], shard.dtype),
            shape(vectors.shape, vectors.dtype),
            shape(ids.shape, ids.dtype),
            shape(noise.shape, noise.dtype),
            shape((GROUPS,) + meta.shape, meta.dtype),
            shape((GROUPS,) + green.shape, green.dtype),
        ),
        in_specs=[spec] * 6,
        out_specs=(spec,) * 6,
        scratch_shapes=[
            pltpu.SemaphoreType.DMA((3,)),
            pltpu.SemaphoreType.DMA((streams, 3, 4)),
            pltpu.SemaphoreType.DMA((streams, 3, 4)),
            pltpu.SemaphoreType.DMA((3,)),
            pltpu.SemaphoreType.DMA((3,)),
            pltpu.SemaphoreType.DMA((2, 3)),
            pltpu.SemaphoreType.DMA((2, 3)),
        ],
        compiler_params=pltpu.CompilerParams(collective_id=0, has_side_effects=True),
        name="gather_green",
    )(shard, vectors, ids, noise, meta, green)


WALKERS_HERE = 8
CHUNK = 4


def diagonal(block, masks):
    merged = block[0:16]
    for r in range(1, 8):
        merged = jnp.where(masks[r], block[16 * r : 16 * r + 16], merged)
    return merged


def contract_kernel(ids_a, ids_b, vec_a, vec_b, green, noise, bias_ref, part_ref, acc, diag):
    vectors = vec_a.shape[0]
    acc[...] = jnp.zeros_like(acc)
    lane16 = lax.broadcasted_iota(jnp.int32, (16, 128), 1)
    masks = [(lane16 // 16) == r for r in range(8)]

    def half(ids, vec, offset):
        def step(turn, carry):
            for w in range(WALKERS_HERE):
                lefts, rights = [], []
                for k in range(CHUNK):
                    g = turn * CHUNK + k
                    rows = []
                    for j in range(2):
                        b = ids[2 * g + j]
                        rows.append(green[w % 4, (w // 4) * 2 + (b // 2) % 2, b // 4, b % 2])
                    tee = jnp.dot(
                        vec[g], jnp.concatenate(rows, 0), preferred_element_type=F32
                    ).astype(BF16)
                    real, imag = tee[:, :128], tee[:, 128:]
                    diag[w, 0, offset + g] = diagonal(real, masks)
                    diag[w, 1, offset + g] = diagonal(imag, masks)
                    lefts.append(tee)
                    rights += [tee, jnp.concatenate([-imag, real], 1)]
                acc[w] += jnp.dot(
                    jnp.concatenate(lefts, 1), jnp.concatenate(rights, 0), preferred_element_type=F32
                )
            return carry

        lax.fori_loop(0, vectors // CHUNK, step, 0)

    half(ids_a, vec_a, 0)
    half(ids_b, vec_b, vectors)

    total = 2 * vectors
    keep = (lax.broadcasted_iota(jnp.int32, (1, 16, 128), 2) % 16) == lax.broadcasted_iota(
        jnp.int32, (1, 16, 128), 1
    )
    block = 16
    span = lax.broadcasted_iota(jnp.int32, (block, block * 16), 1) // 16
    pick = (span == lax.broadcasted_iota(jnp.int32, (block, block * 16), 0)).astype(BF16)
    row16 = lax.broadcasted_iota(jnp.int32, (16, 128), 0)
    bias = jnp.zeros((16, total), F32)
    for w in range(WALKERS_HERE):
        for c in range(2):
            pieces = []
            for p in range(total // block):
                part = diag[w, c, p * block : (p + 1) * block]
                part = jnp.where(keep, part, jnp.zeros_like(part)).reshape(block * 16, 128)
                pieces.append(jnp.dot(pick, part, preferred_element_type=F32).astype(BF16))
            sums = jnp.concatenate(pieces, 0)
            ones = (row16 == c * 8 + w).astype(BF16)
            bias += lax.dot_general(ones, sums, (((1,), (1,)), ((), ())), preferred_element_type=F32)
    bias = 2.0 * bias
    bias_ref[...] = bias
    eye = lax.broadcasted_iota(jnp.int32, (128, 128), 0) == lax.broadcasted_iota(jnp.int32, (128, 128), 1)
    row8 = lax.broadcasted_iota(jnp.int32, (8, 128), 0)
    kx = [jnp.zeros((8, 128), F32), jnp.zeros((8, 128), F32)]
    for w in range(WALKERS_HERE):
        for c in range(2):
            square = acc[w, :, c * 128 : (c + 1) * 128]
            line = jnp.sum(jnp.where(eye, square, 0.0), axis=0, keepdims=True)
            kx[c] += jnp.where(row8 == w, line, 0.0)
    re, im = bias[:8], bias[8:]
    fields = noise[...]
    energy_re = 0.5 * (re * re - im * im) - kx[0]
    energy_im = re * im - kx[1]
    shift_re, shift_im = -ROOT * re, -ROOT * im
    phase_re = fields * shift_re - 0.5 * (shift_re * shift_re - shift_im * shift_im)
    phase_im = fields * shift_im - shift_re * shift_im
    lane8 = lax.broadcasted_iota(jnp.int32, (8, 128), 1)
    result = jnp.zeros((8, 128), F32)
    for i, value in enumerate((energy_re, energy_im, phase_re, phase_im)):
        result = jnp.where(lane8 == i, jnp.sum(value, axis=1, keepdims=True), result)
    part_ref[...] = result


def contract(ids_a, ids_b, vec_a, vec_b, green, noise):
    smem = pl.BlockSpec(memory_space=pltpu.SMEM)
    vmem = pl.BlockSpec(memory_space=pltpu.VMEM)
    vectors = vec_a.shape[0]
    return pl.pallas_call(
        contract_kernel,
        out_shape=(
            jax.ShapeDtypeStruct((16, 2 * vectors), F32),
            jax.ShapeDtypeStruct((8, 128), F32),
        ),
        in_specs=[smem, smem, vmem, vmem, vmem, vmem],
        out_specs=(vmem, vmem),
        scratch_shapes=[
            pltpu.VMEM((WALKERS_HERE, 128, 256), F32),
            pltpu.VMEM((WALKERS_HERE, 2, 2 * vectors, 16, 128), BF16),
        ],
        compiler_params=pltpu.CompilerParams(vmem_limit_bytes=56 * MB),
        name="tee_and_traces",
    )(ids_a, ids_b, vec_a, vec_b, green, noise)


def reduce_kernel(
    part, bias, total_ref, bias2_ref, slots, slots2, own2,
    bias_send, bias_recv, send_sem, recv_sem, send2, recv2,
):
    x, y, z, core = position()
    sibling = device(x, y, z, 1 - core)
    plane = [
        device((x + i) % 4, (y + j) % 4, z, core)
        for i in range(4) for j in range(4) if i + j > 0
    ]
    column = [
        device(x, y, (z + i) % 4, (core + k) % 2)
        for k in range(2) for i in range(4) if i + k > 0
    ]
    barrier = pltpu.get_barrier_semaphore()
    for target in plane + column:
        pl.semaphore_signal(barrier, inc=1, device_id=target, device_id_type=MESH)
    me = x * 4 + y
    me2 = core * 4 + z
    slots[me] = part[...]
    pl.semaphore_wait(barrier, len(plane) + len(column))

    def remote(source, target, send, recv, where):
        return pltpu.make_async_remote_copy(
            src_ref=source, dst_ref=target, send_sem=send, recv_sem=recv,
            device_id=where, device_id_type=MESH,
        )

    first = [
        remote(part, slots.at[me], send_sem.at[i], recv_sem.at[i], target)
        for i, target in enumerate(plane)
    ]
    for copy in first:
        copy.start()
    swap = remote(bias, bias2_ref, bias_send, bias_recv, sibling)
    swap.start()
    for copy in first:
        copy.wait()
    mine = jnp.sum(slots[...], axis=0)
    own2[...] = mine
    slots2[me2] = mine
    second = [
        remote(own2, slots2.at[me2], send2.at[i], recv2.at[i], target)
        for i, target in enumerate(column)
    ]
    for copy in second:
        copy.start()
    for copy in second:
        copy.wait()
    total_ref[0] = jnp.sum(slots2[0:4], axis=0)
    total_ref[1] = jnp.sum(slots2[4:8], axis=0)
    swap.wait()


def reduce_all(part, bias):
    vmem = pl.BlockSpec(memory_space=pltpu.VMEM)
    return pl.pallas_call(
        reduce_kernel,
        out_shape=(
            jax.ShapeDtypeStruct((2, 8, 128), F32),
            jax.ShapeDtypeStruct(bias.shape, F32),
        ),
        in_specs=[vmem, vmem],
        out_specs=(vmem, vmem),
        scratch_shapes=[
            pltpu.VMEM((16, 8, 128), F32),
            pltpu.VMEM((8, 8, 128), F32),
            pltpu.VMEM((8, 128), F32),
            pltpu.SemaphoreType.DMA(()),
            pltpu.SemaphoreType.DMA(()),
            pltpu.SemaphoreType.DMA((15,)),
            pltpu.SemaphoreType.DMA((15,)),
            pltpu.SemaphoreType.DMA((7,)),
            pltpu.SemaphoreType.DMA((7,)),
        ],
        compiler_params=pltpu.CompilerParams(collective_id=1, has_side_effects=True),
        name="reduce_terms",
    )(part, bias)


def body(green, chol_blocks, block_ids, noise, weights, copies, owners):
    grp = lax.axis_index("grp")
    core = grp % 2
    rows, _, _, electrons = green.shape
    vectors = chol_blocks.shape[0]
    shard = jnp.transpose(green, (2, 0, 1, 3)).reshape(WG, rows, 2 * electrons)
    ids = block_ids.reshape(-1)
    meta = jnp.concatenate(
        [weights[:, None], copies[:, None].astype(F32), owners.astype(F32)], axis=1
    )
    meta = jnp.pad(meta, ((0, 4), (0, 128 - 6)))
    gathered, vectors2, ids2, noise2, meta_all, green_all = gather(
        shard, chol_blocks, ids.reshape(1, -1), noise, meta, green
    )
    meta_all = meta_all[:, :WG].reshape(GROUPS * WG, -1)
    all_weights = meta_all[:, 0]
    all_copies = meta_all[:, 1].astype(jnp.int32)
    all_owners = meta_all[:, 2:6].astype(jnp.int32)
    kept = jnp.arange(KMAX, dtype=jnp.int32)[None, :] < all_copies[:, None]
    targets = jnp.arange(GROUPS, dtype=jnp.int32)
    hits = ((all_owners[:, :, None] == targets[None, None, :]) & kept[:, :, None]).astype(jnp.int32)
    hits = hits.reshape(GROUPS * WG * KMAX, GROUPS)
    ranks = jnp.cumsum(hits, axis=0, dtype=jnp.int32) - hits
    slots = jnp.sum(hits * (ranks + targets[None, :] * WG), axis=1, dtype=jnp.int32)
    live = jnp.sum(hits, axis=1, dtype=jnp.int32) > 0
    own_slots = grp * WG + jnp.arange(WG, dtype=jnp.int32)
    route = ((slots[:, None] == own_slots[None, :]) & live[:, None]).astype(F32)
    route = jnp.sum(route.reshape(GROUPS * WG, KMAX, WG), axis=1)
    moved_green = jnp.einsum(
        "gmcwn,gws->mcsn", green_all, route.reshape(GROUPS, WG, WG).astype(BF16),
        preferred_element_type=F32,
    ).astype(BF16)

    def mine(fields):
        return lax.dynamic_index_in_dim(
            fields.reshape(2, 2, WG, vectors), core, axis=1, keepdims=False
        ).reshape(WALKERS_HERE, vectors)

    fields = jnp.concatenate([mine(noise), mine(noise2)], axis=1)
    blocks = gathered.reshape(WG, 4, 4, 2, 2 * rows, 2 * electrons)
    bias, part = contract(ids, ids2.reshape(-1), chol_blocks, vectors2, blocks, fields)
    total, bias2 = reduce_all(part, bias)
    terms = jnp.transpose(total[:, :, :4].reshape(2, 2, WG, 4), (3, 1, 0, 2)).reshape(4, GROUPS * WG)
    every_weight = all_weights * jnp.exp(terms[2]) * jnp.maximum(jnp.cos(terms[3]), 0.0)
    energy = lax.dynamic_slice_in_dim(terms[:2], grp * WG, WG, axis=1)
    new_weights = lax.dynamic_slice_in_dim(every_weight, grp * WG, WG, axis=0)
    moved_weights = jnp.sum(route * every_weight[:, None], axis=0)
    ours = bias[:, :vectors].reshape(2, 2, WG, vectors)
    theirs = bias2[:, vectors:].reshape(2, 2, WG, vectors)
    force_bias = jnp.where(
        core == 0, jnp.stack([ours, theirs], axis=2), jnp.stack([theirs, ours], axis=2)
    ).reshape(2, GROUPS * WG, vectors)
    return (force_bias, energy, new_weights, moved_green, moved_weights)


def solution(mesh):
    return jax.shard_map(
        body,
        mesh=mesh,
        in_specs=(
            P("chol", None, "grp", None),
            P(("grp", "chol"), None, None),
            P(("grp", "chol"), None),
            P(None, ("grp", "chol")),
            P("grp"),
            P("grp"),
            P("grp", None),
        ),
        out_specs=(
            P(None, None, ("grp", "chol")),
            P(None, "grp"),
            P("grp"),
            P("chol", None, "grp", None),
            P("grp"),
        ),
        check_vma=False,
    )
```

```python
import functools
import math

import jax
import jax.numpy as jnp
from jax import lax
from jax.experimental import pallas as pl
from jax.experimental.pallas import tpu as pltpu
from jax.sharding import PartitionSpec as P

MESH = pl.DeviceIdType.MESH
BF16 = jnp.bfloat16
F32 = jnp.float32
KMAX = 4
GROUPS = 4
WG = 4
ROOT = math.sqrt(0.005)
MB = 2**20

def position():
    grp = lax.axis_index("grp")
    chol = lax.axis_index("chol")
    x = (grp // 2) * 2 + (chol // 4) % 2
    return x, chol // 8, chol % 4, grp % 2


def device(x, y, z, core):
    return ((x // 2) * 2 + core, y * 8 + (x % 2) * 4 + z)


STREAMS = (
    (0, (0, 16), (0, 256), "xyz"),
    (0, (16, 16), (0, 128), "yzx"),
    (0, (16, 16), (128, 128), "zxy"),
    (1, (0, 32), (0, 256), "yzx"),
    (2, (0, 32), (0, 256), "zxy"),
    (3, (0, 32), (0, 256), "xyz"),
)
STEP = 16


def diagonal(block, masks, keep):
    merged = block[0:16]
    for r in range(1, 8):
        merged = jnp.where(masks[r], block[16 * r : 16 * r + 16], merged)
    return jnp.sum(jnp.where(keep, merged, jnp.zeros_like(merged)).astype(F32), axis=0, keepdims=True)


def fused_kernel(
    shard, vectors, ids, noise, meta, green,
    total_ref, bias_ref, bias2_ref, meta_all, green_all,
    g0, g1, g2, g3, vec, ids_v, ids_s, noise2, acc, diag, part, slots, slots2, own2,
    local_sem, send_sem, recv_sem, pair_send, pair_recv, group_send, group_recv,
    send1, recv1, send2, recv2,
):
    chunks = (g0, g1, g2, g3)
    x, y, z, core = position()
    grp = lax.axis_index("grp")
    count = vectors.shape[0]
    here = {"x": x, "y": y, "z": z}
    sibling = device(x, y, z, 1 - core)
    across = [device((x + 2) % 4, y, z, core), device((x + 2) % 4, y, z, 1 - core)]
    plane = [
        device((x + i) % 4, (y + j) % 4, z, core)
        for i in range(4) for j in range(4) if i + j > 0
    ]
    column = [
        device(x, y, (z + i) % 4, (core + k) % 2)
        for k in range(2) for i in range(4) if i + k > 0
    ]
    everyone = plane + column + [across[1]]
    barrier = pltpu.get_barrier_semaphore()
    for target in everyone:
        pl.semaphore_signal(barrier, inc=1, device_id=target, device_id_type=MESH)

    local = [
        pltpu.make_async_copy(vectors, vec.at[pl.ds(0, count)], local_sem.at[0]),
        pltpu.make_async_copy(ids, ids_s.at[pl.ds(0, count)], local_sem.at[1]),
        pltpu.make_async_copy(meta, meta_all.at[grp], local_sem.at[2]),
        pltpu.make_async_copy(green, green_all.at[grp], local_sem.at[3]),
    ]
    for copy in local:
        copy.start()
    for c in range(4):
        chunks[c][x, y, z] = shard[c]
    acc[...] = jnp.zeros_like(acc)
    pl.semaphore_wait(barrier, len(everyone))

    def remote(source, target, send, recv, where):
        return pltpu.make_async_remote_copy(
            src_ref=source, dst_ref=target, send_sem=send, recv_sem=recv,
            device_id=where, device_id_type=MESH,
        )

    def move(stream, phase, kind):
        chunk, rows, cols, order = STREAMS[stream]
        axis, free = order[phase], order[:phase]
        up, down, far = dict(here), dict(here), dict(here)
        up[axis] = (here[axis] + 1) % 4
        down[axis] = (here[axis] + 3) % 4
        far[axis] = (here[axis] + 2) % 4
        at, to, span = here, (up, down, far)[kind % 3], slice(None)
        if phase == 2 and kind == 2:
            at, to, span = down, up, pl.ds(0, 2)
        if phase == 2 and kind == 3:
            at, to, span = up, down, pl.ds(2, 2)
        index = [(span if a == order[0] else slice(None)) if a in free else at[a] for a in "xyz"]
        ref = chunks[chunk].at[(*index, pl.ds(*rows), pl.ds(*cols))]
        return remote(
            ref, ref, send_sem.at[stream, phase, kind], recv_sem.at[stream, phase, kind],
            device(to["x"], to["y"], to["z"], core),
        )

    def begin(stream, phase):
        for kind in (0, 1) if phase == 2 else (0, 1, 2):
            move(stream, phase, kind).start()

    def arrive(stream, phase):
        for kind in range(3):
            move(stream, phase, kind).wait_recv()

    def forward(stream):
        move(stream, 2, 0).wait_recv()
        move(stream, 2, 2).start()
        move(stream, 2, 1).wait_recv()
        move(stream, 2, 3).start()

    def finish(stream):
        move(stream, 2, 2).wait_recv()
        move(stream, 2, 3).wait_recv()
        for phase in range(3):
            for kind in range(4 if phase == 2 else 3):
                move(stream, phase, kind).wait_send()

    swaps = [
        remote(ids, ids_v, pair_send.at[0], pair_recv.at[0], sibling),
        remote(noise, noise2, pair_send.at[1], pair_recv.at[1], sibling),
        remote(vectors, vec.at[pl.ds(count, count)], pair_send.at[2], pair_recv.at[2], sibling),
    ]
    groups = []
    for i, target in enumerate([sibling] + across):
        groups.append(remote(meta, meta_all.at[grp], group_send.at[0, i], group_recv.at[0, i], target))
        groups.append(remote(green, green_all.at[grp], group_send.at[1, i], group_recv.at[1, i], target))

    first = (0, 1, 2)
    for s in first:
        begin(s, 0)
    for copy in swaps:
        copy.start()
    for phase in (1, 2):
        for s in first:
            arrive(s, phase - 1)
            begin(s, phase)
    for s in (3, 4, 5):
        begin(s, 0)
    for s in first:
        forward(s)
    for copy in groups:
        copy.start()
    swaps[0].wait()
    ids_copy = pltpu.make_async_copy(ids_v, ids_s.at[pl.ds(count, count)], local_sem.at[4])
    ids_copy.start()
    for copy in local:
        copy.wait()
    ids_copy.wait()
    for s in first:
        finish(s)

    def advance(streams, phase):
        def run():
            for s in streams:
                arrive(s, phase - 1)
                begin(s, phase)
        return run

    def onward(streams):
        def run():
            for s in streams:
                forward(s)
        return run

    events = {
        0: advance((3,), 1),
        1: advance((4, 5), 1),
        2: advance((3,), 2),
        3: advance((4, 5), 2),
        4: lambda: swaps[2].wait(),
        6: onward((3,)),
        7: onward((4, 5)),
    }

    lane16 = lax.broadcasted_iota(jnp.int32, (16, 128), 1)
    masks = [(lane16 // 16) == r for r in range(8)]
    keep = (lane16 % 16) == lax.broadcasted_iota(jnp.int32, (16, 128), 0)

    def compute(chunk, actions):
        ref = chunks[chunk]

        def step(turn, carry):
            for when, action in actions.items():
                pl.when(turn == when)(action)
            places = []
            for k in range(STEP):
                g = turn * STEP + k
                for j in range(2):
                    b = ids_s[g, j]
                    places.append((lax.rem(lax.div(b, 2), 2), lax.div(b, 4), lax.rem(b, 2) * 2))
            for xh in range(2):
                w = xh * 4 + chunk
                lefts, rights = [], []
                for k in range(STEP):
                    g = turn * STEP + k
                    rows = [
                        ref[xh * 2 + px, py, pl.ds(pz, 2)].reshape(64, 256)
                        for px, py, pz in places[2 * k : 2 * k + 2]
                    ]
                    tee = jnp.dot(
                        vec[g], jnp.concatenate(rows, 0), preferred_element_type=F32
                    ).astype(BF16)
                    real, imag = tee[:, :128], tee[:, 128:]
                    diag[w, pl.ds(g, 1)] = diagonal(real, masks, keep)
                    diag[8 + w, pl.ds(g, 1)] = diagonal(imag, masks, keep)
                    lefts.append(tee)
                    rights += [tee, jnp.concatenate([-imag, real], 1)]
                acc[w] += jnp.dot(
                    jnp.concatenate(lefts, 1), jnp.concatenate(rights, 0), preferred_element_type=F32
                )
            return carry

        lax.fori_loop(0, 2 * count // STEP, step, 0)

    compute(0, events)
    for chunk in (1, 2, 3):
        finish(chunk + 2)
        compute(chunk, {})

    row16 = lax.broadcasted_iota(jnp.int32, (16, 128), 0)
    bias = jnp.zeros((16, 2 * count), F32)
    for r in range(16):
        bias += lax.dot_general(
            (row16 == r).astype(BF16), diag[r].astype(BF16),
            (((1,), (1,)), ((), ())), preferred_element_type=F32,
        )
    bias = 2.0 * bias
    bias_ref[...] = bias
    eye = lax.broadcasted_iota(jnp.int32, (128, 128), 0) == lax.broadcasted_iota(jnp.int32, (128, 128), 1)
    row8 = lax.broadcasted_iota(jnp.int32, (8, 128), 0)
    kx = [jnp.zeros((8, 128), F32), jnp.zeros((8, 128), F32)]
    for w in range(8):
        for c in range(2):
            line = jnp.sum(
                jnp.where(eye, acc[w, :, c * 128 : (c + 1) * 128], 0.0), axis=0, keepdims=True
            )
            kx[c] += jnp.where(row8 == w, line, 0.0)
    swaps[1].wait()

    def fields_of(ref):
        return jnp.concatenate(
            [jnp.where(core == 0, ref[0:4], ref[4:8]), jnp.where(core == 0, ref[8:12], ref[12:16])], 0
        )

    fields = jnp.concatenate([fields_of(noise), fields_of(noise2)], 1)
    re, im = bias[:8], bias[8:]
    energy_re = 0.5 * (re * re - im * im) - kx[0]
    energy_im = re * im - kx[1]
    shift_re, shift_im = -ROOT * re, -ROOT * im
    phase_re = fields * shift_re - 0.5 * (shift_re * shift_re - shift_im * shift_im)
    phase_im = fields * shift_im - shift_re * shift_im
    lane8 = lax.broadcasted_iota(jnp.int32, (8, 128), 1)
    result = jnp.zeros((8, 128), F32)
    for i, value in enumerate((energy_re, energy_im, phase_re, phase_im)):
        result = jnp.where(lane8 == i, jnp.sum(value, axis=1, keepdims=True), result)
    part[...] = result

    me = x * 4 + y
    me2 = core * 4 + z
    slots[me] = result
    round1 = [
        remote(part, slots.at[me], send1.at[i], recv1.at[i], target)
        for i, target in enumerate(plane)
    ]
    for copy in round1:
        copy.start()
    swap = remote(bias_ref, bias2_ref, pair_send.at[3], pair_recv.at[3], sibling)
    swap.start()
    for copy in groups:
        copy.wait()
    for copy in round1:
        copy.wait()
    mine = jnp.sum(slots[...], axis=0)
    own2[...] = mine
    slots2[me2] = mine
    round2 = [
        remote(own2, slots2.at[me2], send2.at[i], recv2.at[i], target)
        for i, target in enumerate(column)
    ]
    for copy in round2:
        copy.start()
    for copy in round2:
        copy.wait()
    total_ref[0] = jnp.sum(slots2[0:4], axis=0)
    total_ref[1] = jnp.sum(slots2[4:8], axis=0)
    swap.wait()


def fused(shard, vectors, ids, noise, meta, green):
    vmem = pl.BlockSpec(memory_space=pltpu.VMEM)
    hbm = pl.BlockSpec(memory_space=pl.ANY)
    shape = jax.ShapeDtypeStruct
    count = vectors.shape[0]
    dma = pltpu.SemaphoreType.DMA
    streams = len(STREAMS)
    return pl.pallas_call(
        fused_kernel,
        out_shape=(
            shape((2, 8, 128), F32),
            shape((16, 2 * count), F32),
            shape((16, 2 * count), F32),
            shape((GROUPS,) + meta.shape, meta.dtype),
            shape((GROUPS,) + green.shape, green.dtype),
        ),
        in_specs=[vmem, hbm, vmem, vmem, vmem, hbm],
        out_specs=(vmem, vmem, vmem, vmem, hbm),
        scratch_shapes=[pltpu.VMEM((4, 4, 4) + shard.shape[1:], BF16)] * 4
        + [
            pltpu.VMEM((2 * count,) + vectors.shape[1:], BF16),
            pltpu.VMEM(ids.shape, ids.dtype),
            pltpu.SMEM((2 * count, 2), ids.dtype),
            pltpu.VMEM(noise.shape, F32),
            pltpu.VMEM((8, 128, 256), F32),
            pltpu.VMEM((16, 2 * count, 128), F32),
            pltpu.VMEM((8, 128), F32),
            pltpu.VMEM((16, 8, 128), F32),
            pltpu.VMEM((8, 8, 128), F32),
            pltpu.VMEM((8, 128), F32),
            dma((5,)), dma((streams, 3, 4)), dma((streams, 3, 4)),
            dma((4,)), dma((4,)), dma((2, 3)), dma((2, 3)),
            dma((15,)), dma((15,)), dma((7,)), dma((7,)),
        ],
        compiler_params=pltpu.CompilerParams(
            collective_id=0, has_side_effects=True, vmem_limit_bytes=48 * MB
        ),
        name="fused_step",
    )(shard, vectors, ids, noise, meta, green)


def body(green, chol_blocks, block_ids, noise, weights, copies, owners):
    grp = lax.axis_index("grp")
    core = grp % 2
    rows, _, _, electrons = green.shape
    vectors = chol_blocks.shape[0]
    shard = jnp.transpose(green, (2, 0, 1, 3)).reshape(WG, rows, 2 * electrons)
    meta = jnp.concatenate(
        [weights[:, None], copies[:, None].astype(F32), owners.astype(F32)], axis=1
    )
    meta = jnp.pad(meta, ((0, 4), (0, 128 - 6)))
    total, bias, bias2, meta_all, green_all = fused(
        shard, chol_blocks, block_ids, noise, meta, green
    )
    meta_all = meta_all[:, :WG].reshape(GROUPS * WG, -1)
    all_weights = meta_all[:, 0]
    all_copies = meta_all[:, 1].astype(jnp.int32)
    all_owners = meta_all[:, 2:6].astype(jnp.int32)
    kept = jnp.arange(KMAX, dtype=jnp.int32)[None, :] < all_copies[:, None]
    targets = jnp.arange(GROUPS, dtype=jnp.int32)
    hits = ((all_owners[:, :, None] == targets[None, None, :]) & kept[:, :, None]).astype(jnp.int32)
    hits = hits.reshape(GROUPS * WG * KMAX, GROUPS)
    ranks = jnp.cumsum(hits, axis=0, dtype=jnp.int32) - hits
    slots = jnp.sum(hits * (ranks + targets[None, :] * WG), axis=1, dtype=jnp.int32)
    live = jnp.sum(hits, axis=1, dtype=jnp.int32) > 0
    own_slots = grp * WG + jnp.arange(WG, dtype=jnp.int32)
    route = ((slots[:, None] == own_slots[None, :]) & live[:, None]).astype(F32)
    route = jnp.sum(route.reshape(GROUPS * WG, KMAX, WG), axis=1)
    moved_green = jnp.einsum(
        "gmcwn,gws->mcsn", green_all, route.reshape(GROUPS, WG, WG).astype(BF16),
        preferred_element_type=F32,
    ).astype(BF16)

    terms = jnp.transpose(total[:, :, :4].reshape(2, 2, WG, 4), (3, 1, 0, 2)).reshape(4, GROUPS * WG)
    every_weight = all_weights * jnp.exp(terms[2]) * jnp.maximum(jnp.cos(terms[3]), 0.0)
    energy = lax.dynamic_slice_in_dim(terms[:2], grp * WG, WG, axis=1)
    new_weights = lax.dynamic_slice_in_dim(every_weight, grp * WG, WG, axis=0)
    moved_weights = jnp.sum(route * every_weight[:, None], axis=0)
    ours = bias[:, :vectors].reshape(2, 2, WG, vectors)
    theirs = bias2[:, vectors:].reshape(2, 2, WG, vectors)
    force_bias = jnp.where(
        core == 0, jnp.stack([ours, theirs], axis=2), jnp.stack([theirs, ours], axis=2)
    ).reshape(2, GROUPS * WG, vectors)
    return (force_bias, energy, new_weights, moved_green, moved_weights)


def solution(mesh):
    return jax.shard_map(
        body,
        mesh=mesh,
        in_specs=(
            P("chol", None, "grp", None),
            P(("grp", "chol"), None, None),
            P(("grp", "chol"), None),
            P(None, ("grp", "chol")),
            P("grp"),
            P("grp"),
            P("grp", None),
        ),
        out_specs=(
            P(None, None, ("grp", "chol")),
            P(None, "grp"),
            P("grp"),
            P("chol", None, "grp", None),
            P("grp"),
        ),
        check_vma=False,
    )
```

```python
import functools
import math

import jax
import jax.numpy as jnp
from jax import lax
from jax.experimental import pallas as pl
from jax.experimental.pallas import tpu as pltpu
from jax.sharding import PartitionSpec as P

MESH = pl.DeviceIdType.MESH
BF16 = jnp.bfloat16
F32 = jnp.float32
KMAX = 4
GROUPS = 4
WG = 4
ROOT = math.sqrt(0.005)
MB = 2**20

def position():
    grp = lax.axis_index("grp")
    chol = lax.axis_index("chol")
    x = (grp // 2) * 2 + (chol // 4) % 2
    return x, chol // 8, chol % 4, grp % 2


def device(x, y, z, core):
    return ((x // 2) * 2 + core, y * 8 + (x % 2) * 4 + z)


WINDOWS = (((0, 16), (0, 256)), ((16, 16), (0, 128)), ((16, 16), (128, 128)))
ORDERS = ("xyz", "yzx", "zxy")
STREAMS = tuple(
    (chunk, *WINDOWS[i], ORDERS[(chunk + i) % 3]) for chunk in range(4) for i in range(3)
)
STEP = 32


def diagonal(block, masks, keep):
    merged = block[0:16]
    for r in range(1, 8):
        merged = jnp.where(masks[r], block[16 * r : 16 * r + 16], merged)
    return jnp.sum(jnp.where(keep, merged, jnp.zeros_like(merged)).astype(F32), axis=0, keepdims=True)


def fused_kernel(
    shard, vectors, ids, noise, weights, copies, owners,
    force_ref, energy_ref, new_ref, moved_ref, green_ref,
    g0, g1, g2, g3, vec, ids_v, ids_s, noise1, noise2, acc, diag, part, slots, slots2, own2,
    bias1, bias2, shards, w_all, c_all, o_all, w_s, c_s, o_s,
    local_sem, send_sem, recv_sem, pair_send, pair_recv, group_send, group_recv,
    send1, recv1, send2, recv2,
):
    chunks = (g0, g1, g2, g3)
    x, y, z, core = position()
    grp = lax.axis_index("grp")
    count = vectors.shape[0]
    here = {"x": x, "y": y, "z": z}
    sibling = device(x, y, z, 1 - core)
    across = [device((x + 2) % 4, y, z, core), device((x + 2) % 4, y, z, 1 - core)]
    plane = [
        device((x + i) % 4, (y + j) % 4, z, core)
        for i in range(4) for j in range(4) if i + j > 0
    ]
    column = [
        device(x, y, (z + i) % 4, (core + k) % 2)
        for k in range(2) for i in range(4) if i + k > 0
    ]
    everyone = plane + column + [across[1]]
    barrier = pltpu.get_barrier_semaphore()
    for target in everyone:
        pl.semaphore_signal(barrier, inc=1, device_id=target, device_id_type=MESH)

    starts = [
        pltpu.make_async_copy(shard.at[c], chunks[c].at[x, y, z], local_sem.at[c]) for c in range(4)
    ]
    local = [
        pltpu.make_async_copy(vectors, vec.at[pl.ds(0, count)], local_sem.at[4]),
        pltpu.make_async_copy(ids, ids_s.at[0], local_sem.at[5]),
        pltpu.make_async_copy(noise, noise1, local_sem.at[6]),
    ]
    tables = [
        (shard, shards.at[pl.ds(grp * WG, WG)]),
        (weights, w_all.at[grp]),
        (copies, c_all.at[grp]),
        (owners, o_all.at[grp]),
    ]
    local += [
        pltpu.make_async_copy(source, place, local_sem.at[7 + i]) for i, (source, place) in enumerate(tables)
    ]
    for copy in starts + local:
        copy.start()
    acc[...] = jnp.zeros_like(acc)
    for copy in starts:
        copy.wait()
    pl.semaphore_wait(barrier, len(everyone))

    def remote(source, target, send, recv, where):
        return pltpu.make_async_remote_copy(
            src_ref=source, dst_ref=target, send_sem=send, recv_sem=recv,
            device_id=where, device_id_type=MESH,
        )

    def move(stream, phase, kind):
        chunk, rows, cols, order = STREAMS[stream]
        axis, free = order[phase], order[:phase]
        up, down, far = dict(here), dict(here), dict(here)
        up[axis] = (here[axis] + 1) % 4
        down[axis] = (here[axis] + 3) % 4
        far[axis] = (here[axis] + 2) % 4
        at, to, span = here, (up, down, far)[kind % 3], slice(None)
        if phase == 2 and kind == 2:
            at, to, span = down, up, pl.ds(0, 2)
        if phase == 2 and kind == 3:
            at, to, span = up, down, pl.ds(2, 2)
        index = [(span if a == order[0] else slice(None)) if a in free else at[a] for a in "xyz"]
        ref = chunks[chunk].at[(*index, pl.ds(*rows), pl.ds(*cols))]
        return remote(
            ref, ref, send_sem.at[stream, phase, kind], recv_sem.at[stream, phase, kind],
            device(to["x"], to["y"], to["z"], core),
        )

    def begin(stream, phase):
        for kind in (0, 1) if phase == 2 else (0, 1, 2):
            move(stream, phase, kind).start()

    def arrive(stream, phase):
        for kind in range(3):
            move(stream, phase, kind).wait_recv()

    def forward(stream):
        move(stream, 2, 0).wait_recv()
        move(stream, 2, 2).start()
        move(stream, 2, 1).wait_recv()
        move(stream, 2, 3).start()

    def finish(stream):
        move(stream, 2, 2).wait_recv()
        move(stream, 2, 3).wait_recv()
        for phase in range(3):
            for kind in range(4 if phase == 2 else 3):
                move(stream, phase, kind).wait_send()

    swaps = [
        remote(ids, ids_v, pair_send.at[0], pair_recv.at[0], sibling),
        remote(noise, noise2, pair_send.at[1], pair_recv.at[1], sibling),
        remote(vectors, vec.at[pl.ds(count, count)], pair_send.at[2], pair_recv.at[2], sibling),
    ]
    groups = []
    for i, target in enumerate([sibling] + across):
        for j, (source, place) in enumerate(tables):
            groups.append(remote(source, place, group_send.at[j, i], group_recv.at[j, i], target))

    def streams(chunk):
        return range(3 * chunk, 3 * chunk + 3)

    def advance(chunk, phase):
        def run():
            for s in streams(chunk):
                arrive(s, phase - 1)
                begin(s, phase)
        return run

    def onward(chunk):
        def run():
            for s in streams(chunk):
                forward(s)
        return run

    def complete(chunk):
        for s in streams(chunk):
            finish(s)

    for s in streams(0):
        begin(s, 0)
    for copy in swaps:
        copy.start()
    advance(0, 1)()
    advance(0, 2)()
    for s in streams(1):
        begin(s, 0)
    onward(0)()
    swaps[0].wait()
    ids_copy = pltpu.make_async_copy(ids_v, ids_s.at[1], local_sem.at[11])
    ids_copy.start()
    for copy in local:
        copy.wait()
    ids_copy.wait()
    complete(0)

    lane16 = lax.broadcasted_iota(jnp.int32, (16, 128), 1)
    masks = [(lane16 // 16) == r for r in range(8)]
    keep = (lane16 % 16) == lax.broadcasted_iota(jnp.int32, (16, 128), 0)

    def compute(chunk, actions):
        ref = chunks[chunk]

        def step(turn, carry):
            for when, action in actions.items():
                pl.when(turn == when)(action)
            places = []
            part_of = lax.div(turn, count // STEP)
            for k in range(STEP):
                for j in range(2):
                    b = ids_s[part_of, j, lax.rem(turn, count // STEP) * STEP + k]
                    places.append((lax.rem(lax.div(b, 2), 2), lax.div(b, 4), lax.rem(b, 2) * 2))
            for xh in range(2):
                w = xh * 4 + chunk
                lefts, rights = [], []
                for k in range(STEP):
                    g = turn * STEP + k
                    rows = [
                        ref[xh * 2 + px, py, pl.ds(pz, 2)].reshape(64, 256)
                        for px, py, pz in places[2 * k : 2 * k + 2]
                    ]
                    tee = jnp.dot(
                        vec[g], jnp.concatenate(rows, 0), preferred_element_type=F32
                    ).astype(BF16)
                    real, imag = tee[:, :128], tee[:, 128:]
                    diag[w, pl.ds(g, 1)] = diagonal(real, masks, keep)
                    diag[8 + w, pl.ds(g, 1)] = diagonal(imag, masks, keep)
                    lefts.append(tee)
                    rights += [tee, jnp.concatenate([-imag, real], 1)]
                acc[w] += jnp.dot(
                    jnp.concatenate(lefts, 1), jnp.concatenate(rights, 0), preferred_element_type=F32
                )
            return carry

        lax.fori_loop(0, 2 * count // STEP, step, 0)

    for chunk in range(4):
        actions = {}
        if chunk < 3:
            actions = {0: advance(chunk + 1, 1), 1: advance(chunk + 1, 2), 3: onward(chunk + 1)}
        if chunk == 0:
            actions[2] = lambda: swaps[2].wait()
        if chunk == 1:
            for copy in groups:
                copy.start()
        compute(chunk, actions)
        if chunk < 3:
            if chunk < 2:
                for s in streams(chunk + 2):
                    begin(s, 0)
            complete(chunk + 1)

    row16 = lax.broadcasted_iota(jnp.int32, (16, 128), 0)
    bias = jnp.zeros((16, 2 * count), F32)
    for r in range(16):
        bias += lax.dot_general(
            (row16 == r).astype(BF16), diag[r].astype(BF16),
            (((1,), (1,)), ((), ())), preferred_element_type=F32,
        )
    bias = 2.0 * bias
    bias1[...] = bias
    eye = lax.broadcasted_iota(jnp.int32, (128, 128), 0) == lax.broadcasted_iota(jnp.int32, (128, 128), 1)
    row8 = lax.broadcasted_iota(jnp.int32, (8, 128), 0)
    kx = [jnp.zeros((8, 128), F32), jnp.zeros((8, 128), F32)]
    for w in range(8):
        for c in range(2):
            line = jnp.sum(
                jnp.where(eye, acc[w, :, c * 128 : (c + 1) * 128], 0.0), axis=0, keepdims=True
            )
            kx[c] += jnp.where(row8 == w, line, 0.0)
    swaps[1].wait()

    def fields_of(ref):
        return jnp.concatenate(
            [jnp.where(core == 0, ref[0:4], ref[4:8]), jnp.where(core == 0, ref[8:12], ref[12:16])], 0
        )

    fields = jnp.concatenate([fields_of(noise1), fields_of(noise2)], 1)
    re, im = bias[:8], bias[8:]
    energy_re = 0.5 * (re * re - im * im) - kx[0]
    energy_im = re * im - kx[1]
    shift_re, shift_im = -ROOT * re, -ROOT * im
    phase_re = fields * shift_re - 0.5 * (shift_re * shift_re - shift_im * shift_im)
    phase_im = fields * shift_im - shift_re * shift_im
    lane8 = lax.broadcasted_iota(jnp.int32, (8, 128), 1)
    lane_of = ((row8 // 4) * 2 + core) * 4 + row8 % 4
    result = jnp.zeros((8, 128), F32)
    for i, value in enumerate((energy_re, energy_im, phase_re, phase_im)):
        column_sum = jnp.sum(value, axis=1, keepdims=True)
        line = jnp.sum(jnp.where(lane8 == lane_of, column_sum, 0.0), axis=0, keepdims=True)
        result = jnp.where(row8 == i, line, result)
    part[...] = result

    me = x * 4 + y
    me2 = core * 4 + z
    slots[me] = result
    round1 = [
        remote(part, slots.at[me], send1.at[i], recv1.at[i], target)
        for i, target in enumerate(plane)
    ]
    for copy in round1:
        copy.start()
    swap = remote(bias1, bias2, pair_send.at[3], pair_recv.at[3], sibling)
    swap.start()
    for copy in groups:
        copy.wait()
    scalars = [
        pltpu.make_async_copy(source, place, local_sem.at[12 + i])
        for i, (source, place) in enumerate(((w_all, w_s), (c_all, c_s), (o_all, o_s)))
    ]
    for copy in scalars:
        copy.start()
    for copy in scalars:
        copy.wait()
    lane1 = lax.broadcasted_iota(jnp.int32, (1, 128), 1)
    before = jnp.int32(0)
    sources = [jnp.int32(0)] * WG
    weight_line = jnp.zeros((1, 128), F32)
    for w in range(GROUPS * WG):
        live_copies = c_s[w // WG, 0, w % WG]
        weight_line = jnp.where(lane1 == w, w_s[w // WG, 0, w % WG], weight_line)
        for j in range(KMAX):
            hit = jnp.logical_and(j < live_copies, o_s[w // WG, w % WG, j] == grp)
            for s in range(WG):
                sources[s] = jnp.where(jnp.logical_and(hit, before == s), w, sources[s])
            before = before + jnp.where(hit, 1, 0)
    for s in range(WG):
        green_ref[s] = shards[sources[s]]

    for copy in round1:
        copy.wait()
    mine = jnp.sum(slots[...], axis=0)
    own2[...] = mine
    slots2[me2] = mine
    round2 = [
        remote(own2, slots2.at[me2], send2.at[i], recv2.at[i], target)
        for i, target in enumerate(column)
    ]
    for copy in round2:
        copy.start()
    swap.wait()
    theirs = pltpu.roll(bias2[...], 64, 1)[:, :count]
    ours = bias[:, :count]
    for c in range(2):
        for xh in range(2):
            one = ours[c * 8 + xh * 4 : c * 8 + xh * 4 + 4]
            two = theirs[c * 8 + xh * 4 : c * 8 + xh * 4 + 4]
            force_ref[c, xh * 8 : xh * 8 + 8] = jnp.concatenate(
                [jnp.where(core == 0, one, two), jnp.where(core == 0, two, one)], 0
            )
    for copy in round2:
        copy.wait()
    total = jnp.sum(slots2[...], axis=0)
    new = weight_line * jnp.exp(total[2:3]) * jnp.maximum(jnp.cos(total[3:4]), 0.0)
    moved = jnp.zeros((1, 128), F32)
    for s in range(WG):
        picked = jnp.sum(jnp.where(lane1 == sources[s], new, 0.0), axis=1, keepdims=True)
        moved = jnp.where(lane1 == s, picked, moved)
    shifted = jnp.where(row8 == 2, new, total)
    turn_by = lax.rem(128 - grp * WG, 128)
    shifted = pltpu.roll(shifted, turn_by, 1)
    energy_ref[...] = shifted[0:2, :WG]
    new_ref[...] = shifted[2:3, :WG]
    moved_ref[...] = moved[:, :WG]


def fused(shard, vectors, ids, noise, weights, copies, owners):
    vmem = pl.BlockSpec(memory_space=pltpu.VMEM)
    hbm = pl.BlockSpec(memory_space=pl.ANY)
    shape = jax.ShapeDtypeStruct
    count = vectors.shape[0]
    dma = pltpu.SemaphoreType.DMA
    streams = len(STREAMS)
    I32 = jnp.int32
    return pl.pallas_call(
        fused_kernel,
        out_shape=(
            shape((2, GROUPS * WG, count), F32),
            shape((2, WG), F32),
            shape((1, WG), F32),
            shape((1, WG), F32),
            shape(shard.shape, BF16),
        ),
        in_specs=[hbm] * 7,
        out_specs=(vmem,) * 5,
        scratch_shapes=[pltpu.VMEM((4, 4, 4) + shard.shape[1:], BF16)] * 4
        + [
            pltpu.VMEM((2 * count,) + vectors.shape[1:], BF16),
            pltpu.VMEM(ids.shape, I32),
            pltpu.SMEM((2,) + ids.shape, I32),
            pltpu.VMEM(noise.shape, F32),
            pltpu.VMEM(noise.shape, F32),
            pltpu.VMEM((8, 128, 256), F32),
            pltpu.VMEM((16, 2 * count, 128), F32),
            pltpu.VMEM((8, 128), F32),
            pltpu.VMEM((16, 8, 128), F32),
            pltpu.VMEM((8, 8, 128), F32),
            pltpu.VMEM((8, 128), F32),
            pltpu.VMEM((16, 2 * count), F32),
            pltpu.VMEM((16, 2 * count), F32),
            pltpu.VMEM((GROUPS * WG,) + shard.shape[1:], BF16),
            pltpu.VMEM((GROUPS, 1, WG), F32),
            pltpu.VMEM((GROUPS, 1, WG), I32),
            pltpu.VMEM((GROUPS, WG, KMAX), I32),
            pltpu.SMEM((GROUPS, 1, WG), F32),
            pltpu.SMEM((GROUPS, 1, WG), I32),
            pltpu.SMEM((GROUPS, WG, KMAX), I32),
            dma((15,)), dma((streams, 3, 4)), dma((streams, 3, 4)),
            dma((4,)), dma((4,)), dma((4, 3)), dma((4, 3)),
            dma((15,)), dma((15,)), dma((7,)), dma((7,)),
        ],
        compiler_params=pltpu.CompilerParams(
            collective_id=0, has_side_effects=True, vmem_limit_bytes=63 * MB
        ),
        name="fused_step",
    )(shard, vectors, ids, noise, weights, copies, owners)


def body(green, chol_blocks, block_ids, noise, weights, copies, owners):
    rows, _, _, electrons = green.shape
    shard = jnp.transpose(green, (2, 0, 1, 3)).reshape(WG, rows, 2 * electrons)
    force_bias, energy, new_weights, moved_weights, moved = fused(
        shard, chol_blocks, block_ids.T, noise, weights.reshape(1, WG), copies.reshape(1, WG), owners
    )
    moved_green = jnp.transpose(moved.reshape(WG, rows, 2, electrons), (1, 2, 0, 3))
    return (force_bias, energy, new_weights.reshape(WG), moved_green, moved_weights.reshape(WG))


def solution(mesh):
    return jax.shard_map(
        body,
        mesh=mesh,
        in_specs=(
            P("chol", None, "grp", None),
            P(("grp", "chol"), None, None),
            P(("grp", "chol"), None),
            P(None, ("grp", "chol")),
            P("grp"),
            P("grp"),
            P("grp", None),
        ),
        out_specs=(
            P(None, None, ("grp", "chol")),
            P(None, "grp"),
            P("grp"),
            P("chol", None, "grp", None),
            P("grp"),
        ),
        check_vma=False,
    )
```

```python
import functools
import math

import jax
import jax.numpy as jnp
from jax import lax
from jax.experimental import pallas as pl
from jax.experimental.pallas import tpu as pltpu
from jax.sharding import PartitionSpec as P

MESH = pl.DeviceIdType.MESH
BF16 = jnp.bfloat16
F32 = jnp.float32
KMAX = 4
GROUPS = 4
WG = 4
ROOT = math.sqrt(0.005)
MB = 2**20

def position():
    grp = lax.axis_index("grp")
    chol = lax.axis_index("chol")
    x = (grp // 2) * 2 + (chol // 4) % 2
    return x, chol // 8, chol % 4, grp % 2


def device(x, y, z, core):
    return ((x // 2) * 2 + core, y * 8 + (x % 2) * 4 + z)


WINDOWS = (((0, 16), (0, 256)), ((16, 16), (0, 128)), ((16, 16), (128, 128)))
ORDERS = ("xyz", "yzx", "zxy")
STREAMS = tuple(
    (chunk, *WINDOWS[i], ORDERS[(chunk + i) % 3]) for chunk in range(4) for i in range(3)
)
STEP = 32


def diagonal(block, masks, keep):
    merged = block[0:16]
    for r in range(1, 4):
        merged = jnp.where(masks[r], block[16 * r : 16 * r + 16], merged)
    return jnp.sum(jnp.where(keep, merged, jnp.zeros_like(merged)).astype(F32), axis=0, keepdims=True)


def fused_kernel(
    green, vectors, ids, noise, weights, copies, owners,
    force_ref, energy_ref, new_ref, moved_ref, green_ref,
    g0, g1, g2, g3, vec, ids_v, ids_s, noise1, noise2, acc, diag, part, slots, slots2, own2,
    bias1, bias2, green_v, shards, w_all, c_all, o_all, w_s, c_s, o_s,
    local_sem, send_sem, recv_sem, pair_send, pair_recv, group_send, group_recv,
    send1, recv1, send2, recv2,
):
    chunks = (g0, g1, g2, g3)
    x, y, z, core = position()
    grp = lax.axis_index("grp")
    count = vectors.shape[0]
    here = {"x": x, "y": y, "z": z}
    sibling = device(x, y, z, 1 - core)
    across = [device((x + 2) % 4, y, z, core), device((x + 2) % 4, y, z, 1 - core)]
    plane = [
        device((x + i) % 4, (y + j) % 4, z, core)
        for i in range(4) for j in range(4) if i + j > 0
    ]
    column = [
        device(x, y, (z + i) % 4, (core + k) % 2)
        for k in range(2) for i in range(4) if i + k > 0
    ]
    everyone = plane + column + [across[1]]
    barrier = pltpu.get_barrier_semaphore()
    for target in everyone:
        pl.semaphore_signal(barrier, inc=1, device_id=target, device_id_type=MESH)

    load = pltpu.make_async_copy(green, green_v, local_sem.at[0])
    load.start()
    local = [
        pltpu.make_async_copy(vectors, vec.at[pl.ds(0, count)], local_sem.at[4]),
        pltpu.make_async_copy(ids, ids_s.at[0], local_sem.at[5]),
        pltpu.make_async_copy(noise, noise1, local_sem.at[6]),
    ]
    own_shards = shards.at[pl.ds(grp * WG, WG)]
    tables = [
        (own_shards, own_shards),
        (weights, w_all.at[grp]),
        (copies, c_all.at[grp]),
        (owners, o_all.at[grp]),
    ]
    local += [
        pltpu.make_async_copy(source, place, local_sem.at[7 + i]) for i, (source, place) in enumerate(tables) if i
    ]
    for copy in local:
        copy.start()
    acc[...] = jnp.zeros_like(acc)
    load.wait()
    parts = [jnp.swapaxes(green_v[:, c].astype(F32), 0, 1) for c in range(2)]
    for c in range(4):
        row = jnp.concatenate(
            [parts[i][c][:, h * 64 : h * 64 + 64] for h in range(2) for i in range(2)], 1
        ).astype(BF16)
        chunks[c][x, y, z] = row
        shards[grp * WG + c] = row
    pl.semaphore_wait(barrier, len(everyone))

    def remote(source, target, send, recv, where):
        return pltpu.make_async_remote_copy(
            src_ref=source, dst_ref=target, send_sem=send, recv_sem=recv,
            device_id=where, device_id_type=MESH,
        )

    def move(stream, phase, kind):
        chunk, rows, cols, order = STREAMS[stream]
        axis, free = order[phase], order[:phase]
        to = dict(here)
        to[axis] = (here[axis] + (1, 3, 2)[kind]) % 4
        index = [slice(None) if a in free else here[a] for a in "xyz"]
        ref = chunks[chunk].at[(*index, pl.ds(*rows), pl.ds(*cols))]
        return remote(
            ref, ref, send_sem.at[stream, phase, kind], recv_sem.at[stream, phase, kind],
            device(to["x"], to["y"], to["z"], core),
        )

    def streams(chunk):
        return range(3 * chunk, 3 * chunk + 3)

    def begin(chunk, phase):
        for s in streams(chunk):
            for kind in (2, 0, 1):
                move(s, phase, kind).start()

    def arrive(chunk, phase):
        for s in streams(chunk):
            for kind in range(3):
                move(s, phase, kind).wait_recv()

    def advance(chunk, phase):
        arrive(chunk, phase - 1)
        begin(chunk, phase)

    def sent(chunk):
        for s in streams(chunk):
            for phase in range(3):
                for kind in range(3):
                    move(s, phase, kind).wait_send()

    swaps = [
        remote(ids, ids_v, pair_send.at[0], pair_recv.at[0], sibling),
        remote(noise, noise2, pair_send.at[1], pair_recv.at[1], sibling),
        remote(vectors, vec.at[pl.ds(count, count)], pair_send.at[2], pair_recv.at[2], sibling),
    ]
    groups = []
    for i, target in enumerate([sibling] + across):
        for j, (source, place) in enumerate(tables):
            groups.append(remote(source, place, group_send.at[j, i], group_recv.at[j, i], target))

    begin(0, 0)
    for copy in swaps:
        copy.start()
    advance(0, 1)
    advance(0, 2)
    begin(1, 0)
    swaps[0].wait()
    ids_copy = pltpu.make_async_copy(ids_v, ids_s.at[1], local_sem.at[11])
    ids_copy.start()
    for copy in local:
        copy.wait()
    ids_copy.wait()
    advance(1, 1)
    arrive(0, 2)

    def later(*steps):
        def run():
            for step in steps:
                step()
        return run

    def go(chunk, phase):
        return (lambda: advance(chunk, phase)) if phase else (lambda: begin(chunk, 0))

    events = (
        {
            0: later(go(1, 2), go(2, 0)),
            1: later(go(2, 1)),
            2: later(lambda: swaps[2].wait(), go(2, 2), go(3, 0)),
            3: later(go(3, 1)),
        },
        {0: later(go(3, 2)), 1: later(*[copy.start for copy in groups])},
        {},
        {},
    )

    lane16 = lax.broadcasted_iota(jnp.int32, (16, 128), 1)
    masks = [(lane16 % 64) // 16 == r for r in range(4)]
    sign = jnp.where(lax.broadcasted_iota(jnp.int32, (64, 128), 1) < 64, -1.0, 1.0).astype(BF16)

    def times_i(block):
        return pltpu.roll(block, 64, 1) * sign

    keep = (lane16 % 16) == lax.broadcasted_iota(jnp.int32, (16, 128), 0)

    def compute(chunk, actions):
        ref = chunks[chunk]

        def step(turn, carry):
            for when, action in actions.items():
                pl.when(turn == when)(action)
            places = []
            part_of = lax.div(turn, count // STEP)
            for k in range(STEP):
                for j in range(2):
                    b = ids_s[part_of, j, lax.rem(turn, count // STEP) * STEP + k]
                    places.append((lax.rem(lax.div(b, 2), 2), lax.div(b, 4), lax.rem(b, 2) * 2))
            tees = []
            for xh in range(2):
                w = xh * 4 + chunk
                for k in range(STEP):
                    g = turn * STEP + k
                    rows = [
                        ref[xh * 2 + px, py, pl.ds(pz, 2)].reshape(64, 256)
                        for px, py, pz in places[2 * k : 2 * k + 2]
                    ]
                    tee = jnp.dot(
                        vec[g], jnp.concatenate(rows, 0), preferred_element_type=F32
                    ).astype(BF16)
                    diag[w, pl.ds(g, 1)] = diagonal(tee[:64, :128], masks, keep)
                    diag[8 + w, pl.ds(g, 1)] = diagonal(tee[64:, 128:], masks, keep)
                    tees.append(tee)
            for xh in range(2):
                w = xh * 4 + chunk
                left1, right1, left2, right2 = [], [], [], []
                for tee in tees[xh * STEP : (xh + 1) * STEP]:
                    a, b, c, d = tee[:64, :128], tee[:64, 128:], tee[64:, :128], tee[64:, 128:]
                    left1 += [a, d]
                    right1 += [a, times_i(a), d, times_i(d)]
                    left2.append(b)
                    right2 += [c, times_i(c)]
                for i, (left, right) in enumerate(((left1, right1), (left2, right2))):
                    acc[w, i] += jnp.dot(
                        jnp.concatenate(left, 1), jnp.concatenate(right, 0), preferred_element_type=F32
                    )
            return carry

        lax.fori_loop(0, 2 * count // STEP, step, 0)

    for chunk in range(4):
        if chunk:
            arrive(chunk, 2)
        compute(chunk, events[chunk])
    for chunk in range(4):
        sent(chunk)

    row16 = lax.broadcasted_iota(jnp.int32, (16, 128), 0)
    bias = jnp.zeros((16, 2 * count), F32)
    low16 = lane16 < 64
    for r in range(16):
        pick = row16 == jnp.where(low16, r % 8, 8 + r % 8)
        bias += lax.dot_general(
            pick.astype(BF16), diag[r].astype(BF16),
            (((1,), (1,)), ((), ())), preferred_element_type=F32,
        )
    bias = 2.0 * bias
    bias1[...] = bias
    eye = lax.broadcasted_iota(jnp.int32, (64, 128), 0) == (
        lax.broadcasted_iota(jnp.int32, (64, 128), 1) % 64
    )
    row8 = lax.broadcasted_iota(jnp.int32, (8, 128), 0)
    lane8 = lax.broadcasted_iota(jnp.int32, (8, 128), 1)
    lines = jnp.zeros((8, 128), F32)
    for w in range(8):
        square = acc[w, 0] + 2.0 * acc[w, 1]
        line = jnp.sum(jnp.where(eye, square, 0.0), axis=0, keepdims=True)
        lines = jnp.where(row8 == w, line, lines)
    kx = [jnp.where(lane8 < 64, lines, 0.0), jnp.where(lane8 < 64, 0.0, lines)]
    swaps[1].wait()

    def fields_of(ref):
        return jnp.concatenate(
            [jnp.where(core == 0, ref[0:4], ref[4:8]), jnp.where(core == 0, ref[8:12], ref[12:16])], 0
        )

    fields = jnp.concatenate([fields_of(noise1), fields_of(noise2)], 1)
    re, im = bias[:8], bias[8:]
    energy_re = 0.5 * (re * re - im * im) - kx[0]
    energy_im = re * im - kx[1]
    shift_re, shift_im = -ROOT * re, -ROOT * im
    phase_re = fields * shift_re - 0.5 * (shift_re * shift_re - shift_im * shift_im)
    phase_im = fields * shift_im - shift_re * shift_im
    lane_of = ((row8 // 4) * 2 + core) * 4 + row8 % 4
    result = jnp.zeros((8, 128), F32)
    for i, value in enumerate((energy_re, energy_im, phase_re, phase_im)):
        column_sum = jnp.sum(value, axis=1, keepdims=True)
        line = jnp.sum(jnp.where(lane8 == lane_of, column_sum, 0.0), axis=0, keepdims=True)
        result = jnp.where(row8 == i, line, result)
    part[...] = result

    me = x * 4 + y
    me2 = core * 4 + z
    slots[me] = result
    round1 = [
        remote(part, slots.at[me], send1.at[i], recv1.at[i], target)
        for i, target in enumerate(plane)
    ]
    for copy in round1:
        copy.start()
    swap = remote(bias1, bias2, pair_send.at[3], pair_recv.at[3], sibling)
    swap.start()
    for copy in groups:
        copy.wait()
    scalars = [
        pltpu.make_async_copy(source, place, local_sem.at[12 + i])
        for i, (source, place) in enumerate(((w_all, w_s), (c_all, c_s), (o_all, o_s)))
    ]
    for copy in scalars:
        copy.start()
    for copy in scalars:
        copy.wait()
    lane1 = lax.broadcasted_iota(jnp.int32, (1, 128), 1)
    before = jnp.int32(0)
    sources = [jnp.int32(0)] * WG
    weight_line = jnp.zeros((1, 128), F32)
    for w in range(GROUPS * WG):
        live_copies = c_s[w // WG, 0, w % WG]
        weight_line = jnp.where(lane1 == w, w_s[w // WG, 0, w % WG], weight_line)
        for j in range(KMAX):
            hit = jnp.logical_and(j < live_copies, o_s[w // WG, w % WG, j] == grp)
            for s in range(WG):
                sources[s] = jnp.where(jnp.logical_and(hit, before == s), w, sources[s])
            before = before + jnp.where(hit, 1, 0)
    for s in range(WG):
        green_ref[s] = shards[sources[s]]

    for copy in round1:
        copy.wait()
    mine = jnp.sum(slots[...], axis=0)
    own2[...] = mine
    slots2[me2] = mine
    round2 = [
        remote(own2, slots2.at[me2], send2.at[i], recv2.at[i], target)
        for i, target in enumerate(column)
    ]
    for copy in round2:
        copy.start()
    swap.wait()
    theirs = pltpu.roll(bias2[...], 64, 1)[:, :count]
    ours = bias[:, :count]
    for c in range(2):
        for xh in range(2):
            one = ours[c * 8 + xh * 4 : c * 8 + xh * 4 + 4]
            two = theirs[c * 8 + xh * 4 : c * 8 + xh * 4 + 4]
            force_ref[c, xh * 8 : xh * 8 + 8] = jnp.concatenate(
                [jnp.where(core == 0, one, two), jnp.where(core == 0, two, one)], 0
            )
    for copy in round2:
        copy.wait()
    total = jnp.sum(slots2[...], axis=0)
    new = weight_line * jnp.exp(total[2:3]) * jnp.maximum(jnp.cos(total[3:4]), 0.0)
    moved = jnp.zeros((1, 128), F32)
    for s in range(WG):
        picked = jnp.sum(jnp.where(lane1 == sources[s], new, 0.0), axis=1, keepdims=True)
        moved = jnp.where(lane1 == s, picked, moved)
    shifted = jnp.where(row8 == 2, new, total)
    turn_by = lax.rem(128 - grp * WG, 128)
    shifted = pltpu.roll(shifted, turn_by, 1)
    energy_ref[...] = shifted[0:2, :WG]
    new_ref[...] = shifted[2:3, :WG]
    moved_ref[...] = moved[:, :WG]


def fused(green, vectors, ids, noise, weights, copies, owners):
    vmem = pl.BlockSpec(memory_space=pltpu.VMEM)
    hbm = pl.BlockSpec(memory_space=pl.ANY)
    shape = jax.ShapeDtypeStruct
    count = vectors.shape[0]
    block = (green.shape[0], 2 * green.shape[3])
    dma = pltpu.SemaphoreType.DMA
    streams = len(STREAMS)
    I32 = jnp.int32
    return pl.pallas_call(
        fused_kernel,
        out_shape=(
            shape((2, GROUPS * WG, count), F32),
            shape((2, WG), F32),
            shape((1, WG), F32),
            shape((1, WG), F32),
            shape((WG,) + block, BF16),
        ),
        in_specs=[hbm] * 7,
        out_specs=(vmem,) * 5,
        scratch_shapes=[pltpu.VMEM((4, 4, 4) + block, BF16)] * 4
        + [
            pltpu.VMEM((2 * count,) + vectors.shape[1:], BF16),
            pltpu.VMEM(ids.shape, I32),
            pltpu.SMEM((2,) + ids.shape, I32),
            pltpu.VMEM(noise.shape, F32),
            pltpu.VMEM(noise.shape, F32),
            pltpu.VMEM((8, 2, 64, 128), F32),
            pltpu.VMEM((16, 2 * count, 128), F32),
            pltpu.VMEM((8, 128), F32),
            pltpu.VMEM((16, 8, 128), F32),
            pltpu.VMEM((8, 8, 128), F32),
            pltpu.VMEM((8, 128), F32),
            pltpu.VMEM((16, 2 * count), F32),
            pltpu.VMEM((16, 2 * count), F32),
            pltpu.VMEM(green.shape, BF16),
            pltpu.VMEM((GROUPS * WG,) + block, BF16),
            pltpu.VMEM((GROUPS, 1, WG), F32),
            pltpu.VMEM((GROUPS, 1, WG), I32),
            pltpu.VMEM((GROUPS, WG, KMAX), I32),
            pltpu.SMEM((GROUPS, 1, WG), F32),
            pltpu.SMEM((GROUPS, 1, WG), I32),
            pltpu.SMEM((GROUPS, WG, KMAX), I32),
            dma((15,)), dma((streams, 3, 4)), dma((streams, 3, 4)),
            dma((4,)), dma((4,)), dma((4, 3)), dma((4, 3)),
            dma((15,)), dma((15,)), dma((7,)), dma((7,)),
        ],
        compiler_params=pltpu.CompilerParams(
            collective_id=0, has_side_effects=True, vmem_limit_bytes=63 * MB
        ),
        name="fused_step",
    )(green, vectors, ids, noise, weights, copies, owners)


def outputs_kernel(force, energy, new, moved, green, force_ref, energy_ref, new_ref, moved_ref, green_ref):
    force_ref[...] = force[...]
    energy_ref[...] = energy[...]
    new_ref[...] = new[...]
    moved_ref[...] = moved[...]
    wide = green[...].astype(F32)
    for c in range(2):
        part = jnp.concatenate([wide[:, :, h * 128 + c * 64 : h * 128 + c * 64 + 64] for h in range(2)], 2)
        green_ref[:, c] = jnp.swapaxes(part, 0, 1).astype(BF16)


def outputs(force, energy, new, moved, green):
    vmem = pl.BlockSpec(memory_space=pltpu.VMEM)
    slots, rows, columns = green.shape
    shape = jax.ShapeDtypeStruct
    return pl.pallas_call(
        outputs_kernel,
        out_shape=tuple(shape(a.shape, a.dtype) for a in (force, energy, new, moved))
        + (shape((rows, 2, slots, columns // 2), BF16),),
        in_specs=[vmem] * 5,
        out_specs=(vmem,) * 5,
        compiler_params=pltpu.CompilerParams(vmem_limit_bytes=63 * MB),
        name="outputs",
    )(force, energy, new, moved, green)


def body(green, chol_blocks, block_ids, noise, weights, copies, owners):
    force_bias, energy, new_weights, moved_weights, moved_green = outputs(*fused(
        green, chol_blocks, block_ids.T, noise, weights.reshape(1, WG), copies.reshape(1, WG), owners
    ))
    return (force_bias, energy, new_weights.reshape(WG), moved_green, moved_weights.reshape(WG))


def solution(mesh):
    return jax.shard_map(
        body,
        mesh=mesh,
        in_specs=(
            P("chol", None, "grp", None),
            P(("grp", "chol"), None, None),
            P(("grp", "chol"), None),
            P(None, ("grp", "chol")),
            P("grp"),
            P("grp"),
            P("grp", None),
        ),
        out_specs=(
            P(None, None, ("grp", "chol")),
            P(None, "grp"),
            P("grp"),
            P("chol", None, "grp", None),
            P("grp"),
        ),
        check_vma=False,
    )
```

```python
import functools
import math

import jax
import jax.numpy as jnp
from jax import lax
from jax.experimental import pallas as pl
from jax.experimental.pallas import tpu as pltpu
from jax.sharding import PartitionSpec as P

MESH = pl.DeviceIdType.MESH
BF16 = jnp.bfloat16
F32 = jnp.float32
KMAX = 4
GROUPS = 4
WG = 4
ROOT = math.sqrt(0.005)
MB = 2**20

def position():
    grp = lax.axis_index("grp")
    chol = lax.axis_index("chol")
    x = (grp // 2) * 2 + (chol // 4) % 2
    return x, chol // 8, chol % 4, grp % 2


def device(x, y, z, core):
    return ((x // 2) * 2 + core, y * 8 + (x % 2) * 4 + z)


WINDOWS = (((0, 16), (0, 256)), ((16, 16), (0, 128)), ((16, 16), (128, 128)))
ORDERS = ("xyz", "yzx", "zxy")
STREAMS = tuple(
    (chunk, *WINDOWS[i], ORDERS[(chunk + i) % 3]) for chunk in range(4) for i in range(3)
)
STEP = 32


def diagonal(block, masks, keep):
    merged = block[0:16]
    for r in range(1, 4):
        merged = jnp.where(masks[r], block[16 * r : 16 * r + 16], merged)
    return jnp.sum(jnp.where(keep, merged, jnp.zeros_like(merged)).astype(F32), axis=0, keepdims=True)


def fused_kernel(
    green, vectors, ids, noise, weights, copies, owners,
    force_ref, energy_ref, new_ref, moved_ref, green_ref,
    g0, g1, g2, g3, vec, ids_v, ids_s, noise1, noise2, acc, diag, part, slots, slots2, own2,
    bias1, bias2, green_v, shards, w_all, c_all, o_all, w_s, c_s, o_s,
    local_sem, send_sem, recv_sem, pair_send, pair_recv, group_send, group_recv,
    send1, recv1, send2, recv2,
):
    chunks = (g0, g1, g2, g3)
    x, y, z, core = position()
    grp = lax.axis_index("grp")
    count = vectors.shape[0]
    here = {"x": x, "y": y, "z": z}
    sibling = device(x, y, z, 1 - core)
    across = [device((x + 2) % 4, y, z, core), device((x + 2) % 4, y, z, 1 - core)]
    plane = [
        device((x + i) % 4, (y + j) % 4, z, core)
        for i in range(4) for j in range(4) if i + j > 0
    ]
    column = [
        device(x, y, (z + i) % 4, (core + k) % 2)
        for k in range(2) for i in range(4) if i + k > 0
    ]
    everyone = plane + column + [across[1]]
    barrier = pltpu.get_barrier_semaphore()
    for target in everyone:
        pl.semaphore_signal(barrier, inc=1, device_id=target, device_id_type=MESH)

    load = pltpu.make_async_copy(green, green_v, local_sem.at[0])
    load.start()
    local = [
        pltpu.make_async_copy(vectors, vec.at[pl.ds(0, count)], local_sem.at[4]),
        pltpu.make_async_copy(ids, ids_s.at[0], local_sem.at[5]),
        pltpu.make_async_copy(noise, noise1, local_sem.at[6]),
    ]
    own_shards = shards.at[pl.ds(grp * WG, WG)]
    tables = [
        (own_shards, own_shards),
        (weights, w_all.at[grp]),
        (copies, c_all.at[grp]),
        (owners, o_all.at[grp]),
    ]
    local += [
        pltpu.make_async_copy(source, place, local_sem.at[7 + i]) for i, (source, place) in enumerate(tables) if i
    ]
    for copy in local:
        copy.start()
    acc[...] = jnp.zeros_like(acc)
    load.wait()
    parts = [jnp.swapaxes(green_v[:, c].astype(F32), 0, 1) for c in range(2)]
    for c in range(4):
        row = jnp.concatenate(
            [parts[i][c][:, h * 64 : h * 64 + 64] for h in range(2) for i in range(2)], 1
        ).astype(BF16)
        chunks[c][x, y, z] = row
        shards[grp * WG + c] = row
    pl.semaphore_wait(barrier, len(everyone))

    def remote(source, target, send, recv, where):
        return pltpu.make_async_remote_copy(
            src_ref=source, dst_ref=target, send_sem=send, recv_sem=recv,
            device_id=where, device_id_type=MESH,
        )

    def move(stream, phase, kind):
        chunk, rows, cols, order = STREAMS[stream]
        axis, free = order[phase], order[:phase]
        to = dict(here)
        to[axis] = (here[axis] + (1, 3, 2)[kind]) % 4
        index = [slice(None) if a in free else here[a] for a in "xyz"]
        ref = chunks[chunk].at[(*index, pl.ds(*rows), pl.ds(*cols))]
        return remote(
            ref, ref, send_sem.at[stream, phase, kind], recv_sem.at[stream, phase, kind],
            device(to["x"], to["y"], to["z"], core),
        )

    def streams(chunk):
        return range(3 * chunk, 3 * chunk + 3)

    def begin(chunk, phase):
        for s in streams(chunk):
            for kind in (2, 0, 1):
                move(s, phase, kind).start()

    def arrive(chunk, phase):
        for s in streams(chunk):
            for kind in range(3):
                move(s, phase, kind).wait_recv()

    def advance(chunk, phase):
        arrive(chunk, phase - 1)
        begin(chunk, phase)

    def sent(chunk):
        for s in streams(chunk):
            for phase in range(3):
                for kind in range(3):
                    move(s, phase, kind).wait_send()

    swaps = [
        remote(ids, ids_v, pair_send.at[0], pair_recv.at[0], sibling),
        remote(noise, noise2, pair_send.at[1], pair_recv.at[1], sibling),
        remote(vectors, vec.at[pl.ds(count, count)], pair_send.at[2], pair_recv.at[2], sibling),
    ]
    groups = []
    for i, target in enumerate([sibling] + across):
        for j, (source, place) in enumerate(tables):
            groups.append(remote(source, place, group_send.at[j, i], group_recv.at[j, i], target))

    begin(0, 0)
    for copy in swaps:
        copy.start()
    advance(0, 1)
    advance(0, 2)
    for chunk in (1, 2, 3):
        begin(chunk, 0)
    swaps[0].wait()
    ids_copy = pltpu.make_async_copy(ids_v, ids_s.at[1], local_sem.at[11])
    ids_copy.start()
    for copy in local:
        copy.wait()
    ids_copy.wait()
    advance(1, 1)
    arrive(0, 2)

    def later(*steps):
        def run():
            for step in steps:
                step()
        return run

    def go(chunk, phase):
        return lambda: advance(chunk, phase)

    events = (
        {0: go(1, 2), 2: lambda: swaps[2].wait(), 3: go(2, 1)},
        {0: go(2, 2), 1: later(*[copy.start for copy in groups]), 2: go(3, 1)},
        {0: go(3, 2)},
        {},
    )

    lane16 = lax.broadcasted_iota(jnp.int32, (16, 128), 1)
    masks = [(lane16 % 64) // 16 == r for r in range(4)]
    sign = jnp.where(lax.broadcasted_iota(jnp.int32, (64, 128), 1) < 64, -1.0, 1.0).astype(BF16)

    def times_i(block):
        return pltpu.roll(block, 64, 1) * sign

    keep = (lane16 % 16) == lax.broadcasted_iota(jnp.int32, (16, 128), 0)

    def compute(chunk, actions):
        ref = chunks[chunk]

        def step(turn, carry):
            for when, action in actions.items():
                pl.when(turn == when)(action)
            places = []
            part_of = lax.div(turn, count // STEP)
            for k in range(STEP):
                for j in range(2):
                    b = ids_s[part_of, j, lax.rem(turn, count // STEP) * STEP + k]
                    places.append((lax.rem(lax.div(b, 2), 2), lax.div(b, 4), lax.rem(b, 2) * 2))
            tees = []
            for xh in range(2):
                w = xh * 4 + chunk
                for k in range(STEP):
                    g = turn * STEP + k
                    rows = [
                        ref[xh * 2 + px, py, pl.ds(pz, 2)].reshape(64, 256)
                        for px, py, pz in places[2 * k : 2 * k + 2]
                    ]
                    tee = jnp.dot(
                        vec[g], jnp.concatenate(rows, 0), preferred_element_type=F32
                    ).astype(BF16)
                    diag[w, pl.ds(g, 1)] = diagonal(tee[:64, :128], masks, keep)
                    diag[8 + w, pl.ds(g, 1)] = diagonal(tee[64:, 128:], masks, keep)
                    tees.append(tee)
            for xh in range(2):
                w = xh * 4 + chunk
                left1, right1, left2, right2 = [], [], [], []
                for tee in tees[xh * STEP : (xh + 1) * STEP]:
                    a, b, c, d = tee[:64, :128], tee[:64, 128:], tee[64:, :128], tee[64:, 128:]
                    left1 += [a, d]
                    right1 += [a, times_i(a), d, times_i(d)]
                    left2.append(b)
                    right2 += [c, times_i(c)]
                for i, (left, right) in enumerate(((left1, right1), (left2, right2))):
                    acc[w, i] += jnp.dot(
                        jnp.concatenate(left, 1), jnp.concatenate(right, 0), preferred_element_type=F32
                    )
            return carry

        lax.fori_loop(0, 2 * count // STEP, step, 0)

    for chunk in range(4):
        if chunk:
            arrive(chunk, 2)
        compute(chunk, events[chunk])
    for chunk in range(4):
        sent(chunk)

    row16 = lax.broadcasted_iota(jnp.int32, (16, 128), 0)
    bias = jnp.zeros((16, 2 * count), F32)
    low16 = lane16 < 64
    for r in range(16):
        pick = row16 == jnp.where(low16, r % 8, 8 + r % 8)
        bias += lax.dot_general(
            pick.astype(BF16), diag[r].astype(BF16),
            (((1,), (1,)), ((), ())), preferred_element_type=F32,
        )
    bias = 2.0 * bias
    bias1[...] = bias
    eye = lax.broadcasted_iota(jnp.int32, (64, 128), 0) == (
        lax.broadcasted_iota(jnp.int32, (64, 128), 1) % 64
    )
    row8 = lax.broadcasted_iota(jnp.int32, (8, 128), 0)
    lane8 = lax.broadcasted_iota(jnp.int32, (8, 128), 1)
    lines = jnp.zeros((8, 128), F32)
    for w in range(8):
        square = acc[w, 0] + 2.0 * acc[w, 1]
        line = jnp.sum(jnp.where(eye, square, 0.0), axis=0, keepdims=True)
        lines = jnp.where(row8 == w, line, lines)
    kx = [jnp.where(lane8 < 64, lines, 0.0), jnp.where(lane8 < 64, 0.0, lines)]
    swaps[1].wait()

    def fields_of(ref):
        return jnp.concatenate(
            [jnp.where(core == 0, ref[0:4], ref[4:8]), jnp.where(core == 0, ref[8:12], ref[12:16])], 0
        )

    fields = jnp.concatenate([fields_of(noise1), fields_of(noise2)], 1)
    re, im = bias[:8], bias[8:]
    energy_re = 0.5 * (re * re - im * im) - kx[0]
    energy_im = re * im - kx[1]
    shift_re, shift_im = -ROOT * re, -ROOT * im
    phase_re = fields * shift_re - 0.5 * (shift_re * shift_re - shift_im * shift_im)
    phase_im = fields * shift_im - shift_re * shift_im
    lane_of = ((row8 // 4) * 2 + core) * 4 + row8 % 4
    result = jnp.zeros((8, 128), F32)
    for i, value in enumerate((energy_re, energy_im, phase_re, phase_im)):
        column_sum = jnp.sum(value, axis=1, keepdims=True)
        line = jnp.sum(jnp.where(lane8 == lane_of, column_sum, 0.0), axis=0, keepdims=True)
        result = jnp.where(row8 == i, line, result)
    part[...] = result

    me = x * 4 + y
    me2 = core * 4 + z
    slots[me] = result
    round1 = [
        remote(part, slots.at[me], send1.at[i], recv1.at[i], target)
        for i, target in enumerate(plane)
    ]
    for copy in round1:
        copy.start()
    swap = remote(bias1, bias2, pair_send.at[3], pair_recv.at[3], sibling)
    swap.start()
    for copy in groups:
        copy.wait()
    scalars = [
        pltpu.make_async_copy(source, place, local_sem.at[12 + i])
        for i, (source, place) in enumerate(((w_all, w_s), (c_all, c_s), (o_all, o_s)))
    ]
    for copy in scalars:
        copy.start()
    for copy in scalars:
        copy.wait()
    lane1 = lax.broadcasted_iota(jnp.int32, (1, 128), 1)
    before = jnp.int32(0)
    sources = [jnp.int32(0)] * WG
    weight_line = jnp.zeros((1, 128), F32)
    for w in range(GROUPS * WG):
        live_copies = c_s[w // WG, 0, w % WG]
        weight_line = jnp.where(lane1 == w, w_s[w // WG, 0, w % WG], weight_line)
        for j in range(KMAX):
            hit = jnp.logical_and(j < live_copies, o_s[w // WG, w % WG, j] == grp)
            for s in range(WG):
                sources[s] = jnp.where(jnp.logical_and(hit, before == s), w, sources[s])
            before = before + jnp.where(hit, 1, 0)
    for s in range(WG):
        green_ref[s] = shards[sources[s]]

    for copy in round1:
        copy.wait()
    mine = jnp.sum(slots[...], axis=0)
    own2[...] = mine
    slots2[me2] = mine
    round2 = [
        remote(own2, slots2.at[me2], send2.at[i], recv2.at[i], target)
        for i, target in enumerate(column)
    ]
    for copy in round2:
        copy.start()
    swap.wait()
    theirs = pltpu.roll(bias2[...], 64, 1)[:, :count]
    ours = bias[:, :count]
    for c in range(2):
        for xh in range(2):
            one = ours[c * 8 + xh * 4 : c * 8 + xh * 4 + 4]
            two = theirs[c * 8 + xh * 4 : c * 8 + xh * 4 + 4]
            force_ref[c, xh * 8 : xh * 8 + 8] = jnp.concatenate(
                [jnp.where(core == 0, one, two), jnp.where(core == 0, two, one)], 0
            )
    for copy in round2:
        copy.wait()
    total = jnp.sum(slots2[...], axis=0)
    new = weight_line * jnp.exp(total[2:3]) * jnp.maximum(jnp.cos(total[3:4]), 0.0)
    moved = jnp.zeros((1, 128), F32)
    for s in range(WG):
        picked = jnp.sum(jnp.where(lane1 == sources[s], new, 0.0), axis=1, keepdims=True)
        moved = jnp.where(lane1 == s, picked, moved)
    shifted = jnp.where(row8 == 2, new, total)
    turn_by = lax.rem(128 - grp * WG, 128)
    shifted = pltpu.roll(shifted, turn_by, 1)
    energy_ref[...] = shifted[0:2, :WG]
    new_ref[...] = shifted[2:3, :WG]
    moved_ref[...] = moved[:, :WG]


def fused(green, vectors, ids, noise, weights, copies, owners):
    vmem = pl.BlockSpec(memory_space=pltpu.VMEM)
    hbm = pl.BlockSpec(memory_space=pl.ANY)
    shape = jax.ShapeDtypeStruct
    count = vectors.shape[0]
    block = (green.shape[0], 2 * green.shape[3])
    dma = pltpu.SemaphoreType.DMA
    streams = len(STREAMS)
    I32 = jnp.int32
    return pl.pallas_call(
        fused_kernel,
        out_shape=(
            shape((2, GROUPS * WG, count), F32),
            shape((2, WG), F32),
            shape((1, WG), F32),
            shape((1, WG), F32),
            shape((WG,) + block, BF16),
        ),
        in_specs=[hbm] * 7,
        out_specs=(vmem,) * 5,
        scratch_shapes=[pltpu.VMEM((4, 4, 4) + block, BF16)] * 4
        + [
            pltpu.VMEM((2 * count,) + vectors.shape[1:], BF16),
            pltpu.VMEM(ids.shape, I32),
            pltpu.SMEM((2,) + ids.shape, I32),
            pltpu.VMEM(noise.shape, F32),
            pltpu.VMEM(noise.shape, F32),
            pltpu.VMEM((8, 2, 64, 128), F32),
            pltpu.VMEM((16, 2 * count, 128), F32),
            pltpu.VMEM((8, 128), F32),
            pltpu.VMEM((16, 8, 128), F32),
            pltpu.VMEM((8, 8, 128), F32),
            pltpu.VMEM((8, 128), F32),
            pltpu.VMEM((16, 2 * count), F32),
            pltpu.VMEM((16, 2 * count), F32),
            pltpu.VMEM(green.shape, BF16),
            pltpu.VMEM((GROUPS * WG,) + block, BF16),
            pltpu.VMEM((GROUPS, 1, WG), F32),
            pltpu.VMEM((GROUPS, 1, WG), I32),
            pltpu.VMEM((GROUPS, WG, KMAX), I32),
            pltpu.SMEM((GROUPS, 1, WG), F32),
            pltpu.SMEM((GROUPS, 1, WG), I32),
            pltpu.SMEM((GROUPS, WG, KMAX), I32),
            dma((15,)), dma((streams, 3, 4)), dma((streams, 3, 4)),
            dma((4,)), dma((4,)), dma((4, 3)), dma((4, 3)),
            dma((15,)), dma((15,)), dma((7,)), dma((7,)),
        ],
        compiler_params=pltpu.CompilerParams(
            collective_id=0, has_side_effects=True, vmem_limit_bytes=63 * MB
        ),
        name="fused_step",
    )(green, vectors, ids, noise, weights, copies, owners)


def outputs_kernel(force, energy, new, moved, green, force_ref, energy_ref, new_ref, moved_ref, green_ref):
    force_ref[...] = force[...]
    energy_ref[...] = energy[...]
    new_ref[...] = new[...]
    moved_ref[...] = moved[...]
    wide = green[...].astype(F32)
    for c in range(2):
        part = jnp.concatenate([wide[:, :, h * 128 + c * 64 : h * 128 + c * 64 + 64] for h in range(2)], 2)
        green_ref[:, c] = jnp.swapaxes(part, 0, 1).astype(BF16)


def outputs(force, energy, new, moved, green):
    vmem = pl.BlockSpec(memory_space=pltpu.VMEM)
    slots, rows, columns = green.shape
    shape = jax.ShapeDtypeStruct
    return pl.pallas_call(
        outputs_kernel,
        out_shape=tuple(shape(a.shape, a.dtype) for a in (force, energy, new, moved))
        + (shape((rows, 2, slots, columns // 2), BF16),),
        in_specs=[vmem] * 5,
        out_specs=(vmem,) * 5,
        compiler_params=pltpu.CompilerParams(vmem_limit_bytes=63 * MB),
        name="outputs",
    )(force, energy, new, moved, green)


def body(green, chol_blocks, block_ids, noise, weights, copies, owners):
    force_bias, energy, new_weights, moved_weights, moved_green = outputs(*fused(
        green, chol_blocks, block_ids.T, noise, weights.reshape(1, WG), copies.reshape(1, WG), owners
    ))
    return (force_bias, energy, new_weights.reshape(WG), moved_green, moved_weights.reshape(WG))


def solution(mesh):
    return jax.shard_map(
        body,
        mesh=mesh,
        in_specs=(
            P("chol", None, "grp", None),
            P(("grp", "chol"), None, None),
            P(("grp", "chol"), None),
            P(None, ("grp", "chol")),
            P("grp"),
            P("grp"),
            P("grp", None),
        ),
        out_specs=(
            P(None, None, ("grp", "chol")),
            P(None, "grp"),
            P("grp"),
            P("chol", None, "grp", None),
            P("grp"),
        ),
        check_vma=False,
    )
```

```python
import functools
import math

import jax
import jax.numpy as jnp
from jax import lax
from jax.experimental import pallas as pl
from jax.experimental.pallas import tpu as pltpu
from jax.sharding import PartitionSpec as P

MESH = pl.DeviceIdType.MESH
BF16 = jnp.bfloat16
F32 = jnp.float32
KMAX = 4
GROUPS = 4
WG = 4
ROOT = math.sqrt(0.005)
MB = 2**20

def position():
    grp = lax.axis_index("grp")
    chol = lax.axis_index("chol")
    x = (grp // 2) * 2 + (chol // 4) % 2
    return x, chol // 8, chol % 4, grp % 2


def device(x, y, z, core):
    return ((x // 2) * 2 + core, y * 8 + (x % 2) * 4 + z)


WINDOWS = (((0, 16), (0, 256)), ((16, 16), (0, 128)), ((16, 16), (128, 128)))
ORDERS = ("xyz", "yzx", "zxy")
STREAMS = tuple(
    (chunk, *WINDOWS[i], ORDERS[(chunk + i) % 3]) for chunk in range(4) for i in range(3)
)
STEP = 64


def diagonal(block, masks, keep):
    merged = block[0:16]
    for r in range(1, 4):
        merged = jnp.where(masks[r], block[16 * r : 16 * r + 16], merged)
    return jnp.sum(jnp.where(keep, merged, jnp.zeros_like(merged)).astype(F32), axis=0, keepdims=True)


def fused_kernel(
    green, vectors, ids, noise, weights, copies, owners,
    force_ref, energy_ref, new_ref, moved_ref, green_ref,
    g0, g1, g2, g3, vec, ids_v, ids_s, noise1, noise2, acc, diag, part, slots, slots2, own2,
    bias1, bias2, green_v, shards, w_all, c_all, o_all, w_s, c_s, o_s,
    local_sem, send_sem, recv_sem, pair_send, pair_recv, group_send, group_recv,
    send1, recv1, send2, recv2,
):
    chunks = (g0, g1, g2, g3)
    x, y, z, core = position()
    grp = lax.axis_index("grp")
    count = vectors.shape[0]
    here = {"x": x, "y": y, "z": z}
    sibling = device(x, y, z, 1 - core)
    across = [device((x + 2) % 4, y, z, core), device((x + 2) % 4, y, z, 1 - core)]
    plane = [
        device((x + i) % 4, (y + j) % 4, z, core)
        for i in range(4) for j in range(4) if i + j > 0
    ]
    column = [
        device(x, y, (z + i) % 4, (core + k) % 2)
        for k in range(2) for i in range(4) if i + k > 0
    ]
    everyone = plane + column + [across[1]]
    barrier = pltpu.get_barrier_semaphore()
    for target in everyone:
        pl.semaphore_signal(barrier, inc=1, device_id=target, device_id_type=MESH)

    load = pltpu.make_async_copy(green, green_v, local_sem.at[0])
    load.start()
    local = [
        pltpu.make_async_copy(vectors, vec.at[pl.ds(0, count)], local_sem.at[4]),
        pltpu.make_async_copy(ids, ids_s.at[0], local_sem.at[5]),
        pltpu.make_async_copy(noise, noise1, local_sem.at[6]),
    ]
    own_shards = shards.at[pl.ds(grp * WG, WG)]
    tables = [
        (own_shards, own_shards),
        (weights, w_all.at[grp]),
        (copies, c_all.at[grp]),
        (owners, o_all.at[grp]),
    ]
    local += [
        pltpu.make_async_copy(source, place, local_sem.at[7 + i]) for i, (source, place) in enumerate(tables) if i
    ]
    for copy in local:
        copy.start()
    acc[...] = jnp.zeros_like(acc)
    load.wait()
    parts = [jnp.swapaxes(green_v[:, c].astype(F32), 0, 1) for c in range(2)]
    for c in range(4):
        row = jnp.concatenate(
            [parts[i][c][:, h * 64 : h * 64 + 64] for h in range(2) for i in range(2)], 1
        ).astype(BF16)
        chunks[c][x, y, z] = row
        shards[grp * WG + c] = row
    pl.semaphore_wait(barrier, len(everyone))

    def remote(source, target, send, recv, where):
        return pltpu.make_async_remote_copy(
            src_ref=source, dst_ref=target, send_sem=send, recv_sem=recv,
            device_id=where, device_id_type=MESH,
        )

    def move(stream, phase, kind):
        chunk, rows, cols, order = STREAMS[stream]
        axis, free = order[phase], order[:phase]
        to = dict(here)
        to[axis] = (here[axis] + (1, 3, 2)[kind]) % 4
        index = [slice(None) if a in free else here[a] for a in "xyz"]
        ref = chunks[chunk].at[(*index, pl.ds(*rows), pl.ds(*cols))]
        return remote(
            ref, ref, send_sem.at[stream, phase, kind], recv_sem.at[stream, phase, kind],
            device(to["x"], to["y"], to["z"], core),
        )

    def streams(chunk):
        return range(3 * chunk, 3 * chunk + 3)

    def begin(chunk, phase):
        for s in streams(chunk):
            for kind in (2, 0, 1):
                move(s, phase, kind).start()

    def arrive(chunk, phase):
        for s in streams(chunk):
            for kind in range(3):
                move(s, phase, kind).wait_recv()

    def advance(chunk, phase):
        arrive(chunk, phase - 1)
        begin(chunk, phase)

    def sent(chunk):
        for s in streams(chunk):
            for phase in range(3):
                for kind in range(3):
                    move(s, phase, kind).wait_send()

    swaps = [
        remote(ids, ids_v, pair_send.at[0], pair_recv.at[0], sibling),
        remote(noise, noise2, pair_send.at[1], pair_recv.at[1], sibling),
        remote(vectors, vec.at[pl.ds(count, count)], pair_send.at[2], pair_recv.at[2], sibling),
    ]
    groups = []
    for i, target in enumerate([sibling] + across):
        for j, (source, place) in enumerate(tables):
            groups.append(remote(source, place, group_send.at[j, i], group_recv.at[j, i], target))

    begin(0, 0)
    for copy in swaps:
        copy.start()
    advance(0, 1)
    advance(0, 2)
    for chunk in (1, 2, 3):
        begin(chunk, 0)
    swaps[0].wait()
    ids_copy = pltpu.make_async_copy(ids_v, ids_s.at[1], local_sem.at[11])
    ids_copy.start()
    for copy in local:
        copy.wait()
    ids_copy.wait()
    advance(1, 1)
    arrive(0, 2)

    def later(*steps):
        def run():
            for step in steps:
                step()
        return run

    def go(chunk, phase):
        return lambda: advance(chunk, phase)

    events = (
        {0: go(1, 2), 1: later(lambda: swaps[2].wait(), go(2, 1))},
        {0: go(2, 2), 1: later(*[copy.start for copy in groups], go(3, 1))},
        {0: go(3, 2)},
        {},
    )

    lane16 = lax.broadcasted_iota(jnp.int32, (16, 128), 1)
    masks = [(lane16 % 64) // 16 == r for r in range(4)]
    sign = jnp.where(lax.broadcasted_iota(jnp.int32, (64, 128), 1) < 64, -1.0, 1.0).astype(BF16)

    def times_i(block):
        return pltpu.roll(block, 64, 1) * sign

    keep = (lane16 % 16) == lax.broadcasted_iota(jnp.int32, (16, 128), 0)

    def compute(chunk, actions):
        ref = chunks[chunk]

        def step(turn, carry):
            for when, action in actions.items():
                pl.when(turn == when)(action)
            places = []
            part_of = lax.div(turn, count // STEP)
            for k in range(STEP):
                for j in range(2):
                    b = ids_s[part_of, j, lax.rem(turn, count // STEP) * STEP + k]
                    places.append((lax.rem(lax.div(b, 2), 2), lax.div(b, 4), lax.rem(b, 2) * 2))
            tees = []
            for xh in range(2):
                w = xh * 4 + chunk
                for k in range(STEP):
                    g = turn * STEP + k
                    rows = [
                        ref[xh * 2 + px, py, pl.ds(pz, 2)].reshape(64, 256)
                        for px, py, pz in places[2 * k : 2 * k + 2]
                    ]
                    tee = jnp.dot(
                        vec[g], jnp.concatenate(rows, 0), preferred_element_type=F32
                    ).astype(BF16)
                    diag[w, pl.ds(g, 1)] = diagonal(tee[:64, :128], masks, keep)
                    diag[8 + w, pl.ds(g, 1)] = diagonal(tee[64:, 128:], masks, keep)
                    tees.append(tee)
            for xh in range(2):
                w = xh * 4 + chunk
                left1, right1, left2, right2 = [], [], [], []
                for tee in tees[xh * STEP : (xh + 1) * STEP]:
                    a, b, c, d = tee[:64, :128], tee[:64, 128:], tee[64:, :128], tee[64:, 128:]
                    left1 += [a, d]
                    right1 += [a, times_i(a), d, times_i(d)]
                    left2.append(b)
                    right2 += [c, times_i(c)]
                for i, (left, right) in enumerate(((left1, right1), (left2, right2))):
                    acc[w, i] += jnp.dot(
                        jnp.concatenate(left, 1), jnp.concatenate(right, 0), preferred_element_type=F32
                    )
            return carry

        lax.fori_loop(0, 2 * count // STEP, step, 0)

    for chunk in range(4):
        if chunk:
            arrive(chunk, 2)
        compute(chunk, events[chunk])
    row16 = lax.broadcasted_iota(jnp.int32, (16, 128), 0)
    bias = jnp.zeros((16, 2 * count), F32)
    low16 = lane16 < 64
    for r in range(16):
        pick = row16 == jnp.where(low16, r % 8, 8 + r % 8)
        bias += lax.dot_general(
            pick.astype(BF16), diag[r].astype(BF16),
            (((1,), (1,)), ((), ())), preferred_element_type=F32,
        )
    bias = 2.0 * bias
    bias1[...] = bias
    eye = lax.broadcasted_iota(jnp.int32, (64, 128), 0) == (
        lax.broadcasted_iota(jnp.int32, (64, 128), 1) % 64
    )
    row8 = lax.broadcasted_iota(jnp.int32, (8, 128), 0)
    lane8 = lax.broadcasted_iota(jnp.int32, (8, 128), 1)
    lines = jnp.zeros((8, 128), F32)
    for w in range(8):
        square = acc[w, 0] + 2.0 * acc[w, 1]
        line = jnp.sum(jnp.where(eye, square, 0.0), axis=0, keepdims=True)
        lines = jnp.where(row8 == w, line, lines)
    kx = [jnp.where(lane8 < 64, lines, 0.0), jnp.where(lane8 < 64, 0.0, lines)]
    swaps[1].wait()

    def fields_of(ref):
        return jnp.concatenate(
            [jnp.where(core == 0, ref[0:4], ref[4:8]), jnp.where(core == 0, ref[8:12], ref[12:16])], 0
        )

    fields = jnp.concatenate([fields_of(noise1), fields_of(noise2)], 1)
    re, im = bias[:8], bias[8:]
    energy_re = 0.5 * (re * re - im * im) - kx[0]
    energy_im = re * im - kx[1]
    shift_re, shift_im = -ROOT * re, -ROOT * im
    phase_re = fields * shift_re - 0.5 * (shift_re * shift_re - shift_im * shift_im)
    phase_im = fields * shift_im - shift_re * shift_im
    lane_of = ((row8 // 4) * 2 + core) * 4 + row8 % 4
    result = jnp.zeros((8, 128), F32)
    for i, value in enumerate((energy_re, energy_im, phase_re, phase_im)):
        column_sum = jnp.sum(value, axis=1, keepdims=True)
        line = jnp.sum(jnp.where(lane8 == lane_of, column_sum, 0.0), axis=0, keepdims=True)
        result = jnp.where(row8 == i, line, result)
    part[...] = result

    me = x * 4 + y
    me2 = core * 4 + z
    slots[me] = result
    round1 = [
        remote(part, slots.at[me], send1.at[i], recv1.at[i], target)
        for i, target in enumerate(plane)
    ]
    for copy in round1:
        copy.start()
    swap = remote(bias1, bias2, pair_send.at[3], pair_recv.at[3], sibling)
    swap.start()
    for chunk in range(4):
        sent(chunk)
    for copy in groups:
        copy.wait()
    scalars = [
        pltpu.make_async_copy(source, place, local_sem.at[12 + i])
        for i, (source, place) in enumerate(((w_all, w_s), (c_all, c_s), (o_all, o_s)))
    ]
    for copy in scalars:
        copy.start()
    for copy in scalars:
        copy.wait()
    lane1 = lax.broadcasted_iota(jnp.int32, (1, 128), 1)
    before = jnp.int32(0)
    sources = [jnp.int32(0)] * WG
    weight_line = jnp.zeros((1, 128), F32)
    for w in range(GROUPS * WG):
        live_copies = c_s[w // WG, 0, w % WG]
        weight_line = jnp.where(lane1 == w, w_s[w // WG, 0, w % WG], weight_line)
        for j in range(KMAX):
            hit = jnp.logical_and(j < live_copies, o_s[w // WG, w % WG, j] == grp)
            for s in range(WG):
                sources[s] = jnp.where(jnp.logical_and(hit, before == s), w, sources[s])
            before = before + jnp.where(hit, 1, 0)
    for s in range(WG):
        green_ref[s] = shards[sources[s]]

    for copy in round1:
        copy.wait()
    mine = jnp.sum(slots[...], axis=0)
    own2[...] = mine
    slots2[me2] = mine
    round2 = [
        remote(own2, slots2.at[me2], send2.at[i], recv2.at[i], target)
        for i, target in enumerate(column)
    ]
    for copy in round2:
        copy.start()
    swap.wait()
    theirs = pltpu.roll(bias2[...], 64, 1)[:, :count]
    ours = bias[:, :count]
    for c in range(2):
        for xh in range(2):
            one = ours[c * 8 + xh * 4 : c * 8 + xh * 4 + 4]
            two = theirs[c * 8 + xh * 4 : c * 8 + xh * 4 + 4]
            force_ref[c, xh * 8 : xh * 8 + 8] = jnp.concatenate(
                [jnp.where(core == 0, one, two), jnp.where(core == 0, two, one)], 0
            )
    for copy in round2:
        copy.wait()
    total = jnp.sum(slots2[...], axis=0)
    new = weight_line * jnp.exp(total[2:3]) * jnp.maximum(jnp.cos(total[3:4]), 0.0)
    moved = jnp.zeros((1, 128), F32)
    for s in range(WG):
        picked = jnp.sum(jnp.where(lane1 == sources[s], new, 0.0), axis=1, keepdims=True)
        moved = jnp.where(lane1 == s, picked, moved)
    shifted = jnp.where(row8 == 2, new, total)
    turn_by = lax.rem(128 - grp * WG, 128)
    shifted = pltpu.roll(shifted, turn_by, 1)
    energy_ref[...] = shifted[0:2, :WG]
    new_ref[...] = shifted[2:3, :WG]
    moved_ref[...] = moved[:, :WG]


def fused(green, vectors, ids, noise, weights, copies, owners):
    vmem = pl.BlockSpec(memory_space=pltpu.VMEM)
    hbm = pl.BlockSpec(memory_space=pl.ANY)
    shape = jax.ShapeDtypeStruct
    count = vectors.shape[0]
    block = (green.shape[0], 2 * green.shape[3])
    dma = pltpu.SemaphoreType.DMA
    streams = len(STREAMS)
    I32 = jnp.int32
    return pl.pallas_call(
        fused_kernel,
        out_shape=(
            shape((2, GROUPS * WG, count), F32),
            shape((2, WG), F32),
            shape((1, WG), F32),
            shape((1, WG), F32),
            shape((WG,) + block, BF16),
        ),
        in_specs=[hbm] * 7,
        out_specs=(vmem,) * 5,
        scratch_shapes=[pltpu.VMEM((4, 4, 4) + block, BF16)] * 4
        + [
            pltpu.VMEM((2 * count,) + vectors.shape[1:], BF16),
            pltpu.VMEM(ids.shape, I32),
            pltpu.SMEM((2,) + ids.shape, I32),
            pltpu.VMEM(noise.shape, F32),
            pltpu.VMEM(noise.shape, F32),
            pltpu.VMEM((8, 2, 64, 128), F32),
            pltpu.VMEM((16, 2 * count, 128), F32),
            pltpu.VMEM((8, 128), F32),
            pltpu.VMEM((16, 8, 128), F32),
            pltpu.VMEM((8, 8, 128), F32),
            pltpu.VMEM((8, 128), F32),
            pltpu.VMEM((16, 2 * count), F32),
            pltpu.VMEM((16, 2 * count), F32),
            pltpu.VMEM(green.shape, BF16),
            pltpu.VMEM((GROUPS * WG,) + block, BF16),
            pltpu.VMEM((GROUPS, 1, WG), F32),
            pltpu.VMEM((GROUPS, 1, WG), I32),
            pltpu.VMEM((GROUPS, WG, KMAX), I32),
            pltpu.SMEM((GROUPS, 1, WG), F32),
            pltpu.SMEM((GROUPS, 1, WG), I32),
            pltpu.SMEM((GROUPS, WG, KMAX), I32),
            dma((15,)), dma((streams, 3, 4)), dma((streams, 3, 4)),
            dma((4,)), dma((4,)), dma((4, 3)), dma((4, 3)),
            dma((15,)), dma((15,)), dma((7,)), dma((7,)),
        ],
        compiler_params=pltpu.CompilerParams(
            collective_id=0, has_side_effects=True, vmem_limit_bytes=63 * MB
        ),
        name="fused_step",
    )(green, vectors, ids, noise, weights, copies, owners)


def outputs_kernel(force, energy, new, moved, green, force_ref, energy_ref, new_ref, moved_ref, green_ref):
    force_ref[...] = force[...]
    energy_ref[...] = energy[...]
    new_ref[...] = new[...]
    moved_ref[...] = moved[...]
    wide = green[...].astype(F32)
    for c in range(2):
        part = jnp.concatenate([wide[:, :, h * 128 + c * 64 : h * 128 + c * 64 + 64] for h in range(2)], 2)
        green_ref[:, c] = jnp.swapaxes(part, 0, 1).astype(BF16)


def outputs(force, energy, new, moved, green):
    vmem = pl.BlockSpec(memory_space=pltpu.VMEM)
    slots, rows, columns = green.shape
    shape = jax.ShapeDtypeStruct
    return pl.pallas_call(
        outputs_kernel,
        out_shape=tuple(shape(a.shape, a.dtype) for a in (force, energy, new, moved))
        + (shape((rows, 2, slots, columns // 2), BF16),),
        in_specs=[vmem] * 5,
        out_specs=(vmem,) * 5,
        compiler_params=pltpu.CompilerParams(vmem_limit_bytes=63 * MB),
        name="outputs",
    )(force, energy, new, moved, green)


def body(green, chol_blocks, block_ids, noise, weights, copies, owners):
    force_bias, energy, new_weights, moved_weights, moved_green = outputs(*fused(
        green, chol_blocks, block_ids.T, noise, weights.reshape(1, WG), copies.reshape(1, WG), owners
    ))
    return (force_bias, energy, new_weights.reshape(WG), moved_green, moved_weights.reshape(WG))


def solution(mesh):
    return jax.shard_map(
        body,
        mesh=mesh,
        in_specs=(
            P("chol", None, "grp", None),
            P(("grp", "chol"), None, None),
            P(("grp", "chol"), None),
            P(None, ("grp", "chol")),
            P("grp"),
            P("grp"),
            P("grp", None),
        ),
        out_specs=(
            P(None, None, ("grp", "chol")),
            P(None, "grp"),
            P("grp"),
            P("chol", None, "grp", None),
            P("grp"),
        ),
        check_vma=False,
    )
```

```python
import functools
import math

import jax
import jax.numpy as jnp
from jax import lax
from jax.experimental import pallas as pl
from jax.experimental.pallas import tpu as pltpu
from jax.sharding import PartitionSpec as P

MESH = pl.DeviceIdType.MESH
BF16 = jnp.bfloat16
F32 = jnp.float32
KMAX = 4
GROUPS = 4
WG = 4
ROOT = math.sqrt(0.005)
MB = 2**20

def position():
    grp = lax.axis_index("grp")
    chol = lax.axis_index("chol")
    x = (grp // 2) * 2 + (chol // 4) % 2
    return x, chol // 8, chol % 4, grp % 2


def device(x, y, z, core):
    return ((x // 2) * 2 + core, y * 8 + (x % 2) * 4 + z)


WINDOWS = (((0, 16), (0, 256)), ((16, 16), (0, 128)), ((16, 16), (128, 128)))
ORDERS = ("xyz", "yzx", "zxy")
STREAMS = tuple(
    (chunk, *WINDOWS[i], ORDERS[(chunk + i) % 3]) for chunk in range(4) for i in range(3)
)
STEP = 64


def diagonal(block, masks, keep):
    merged = block[0:16]
    for r in range(1, 4):
        merged = jnp.where(masks[r], block[16 * r : 16 * r + 16], merged)
    return jnp.sum(jnp.where(keep, merged, jnp.zeros_like(merged)).astype(F32), axis=0, keepdims=True)


def fused_kernel(
    green, vectors, ids, noise, weights, copies, owners,
    force_ref, energy_ref, new_ref, moved_ref, green_ref,
    g0, g1, g2, g3, vec, ids_v, ids_s, noise1, noise2, acc, diag, part, rounds,
    bias1, bias2, green_v, shards, w_all, c_all, o_all, w_s, c_s, o_s,
    local_sem, send_sem, recv_sem, pair_send, pair_recv, group_send, group_recv,
    send1, recv1,
):
    chunks = (g0, g1, g2, g3)
    x, y, z, core = position()
    grp = lax.axis_index("grp")
    count = vectors.shape[0]
    here = {"x": x, "y": y, "z": z}
    sibling = device(x, y, z, 1 - core)
    across = [device((x + 2) % 4, y, z, core), device((x + 2) % 4, y, z, 1 - core)]
    column = [
        device(x, y, (z + i) % 4, (core + k) % 2)
        for k in range(2) for i in range(4) if i + k > 0
    ]
    everyone = column + [across[1]]
    everyone += [device((x + i) % 4, y, z, core) for i in (1, 2, 3)]
    everyone += [device(x, (y + i) % 4, z, core) for i in (1, 2, 3)]
    barrier = pltpu.get_barrier_semaphore()
    for target in everyone:
        pl.semaphore_signal(barrier, inc=1, device_id=target, device_id_type=MESH)

    load = pltpu.make_async_copy(green, green_v, local_sem.at[0])
    load.start()
    local = [
        pltpu.make_async_copy(vectors, vec.at[pl.ds(0, count)], local_sem.at[4]),
        pltpu.make_async_copy(ids, ids_s.at[0], local_sem.at[5]),
        pltpu.make_async_copy(noise, noise1, local_sem.at[6]),
    ]
    own_shards = shards.at[pl.ds(grp * WG, WG)]
    tables = [
        (own_shards, own_shards),
        (weights, w_all.at[grp]),
        (copies, c_all.at[grp]),
        (owners, o_all.at[grp]),
    ]
    local += [
        pltpu.make_async_copy(source, place, local_sem.at[7 + i]) for i, (source, place) in enumerate(tables) if i
    ]
    for copy in local:
        copy.start()
    acc[...] = jnp.zeros_like(acc)
    load.wait()
    parts = [jnp.swapaxes(green_v[:, c].astype(F32), 0, 1) for c in range(2)]
    for c in range(4):
        row = jnp.concatenate(
            [parts[i][c][:, h * 64 : h * 64 + 64] for h in range(2) for i in range(2)], 1
        ).astype(BF16)
        chunks[c][x, y, z] = row
        shards[grp * WG + c] = row
    pl.semaphore_wait(barrier, len(everyone))

    def remote(source, target, send, recv, where):
        return pltpu.make_async_remote_copy(
            src_ref=source, dst_ref=target, send_sem=send, recv_sem=recv,
            device_id=where, device_id_type=MESH,
        )

    def move(stream, phase, kind):
        chunk, rows, cols, order = STREAMS[stream]
        axis, free = order[phase], order[:phase]
        to = dict(here)
        to[axis] = (here[axis] + (1, 3, 2)[kind]) % 4
        index = [slice(None) if a in free else here[a] for a in "xyz"]
        ref = chunks[chunk].at[(*index, pl.ds(*rows), pl.ds(*cols))]
        return remote(
            ref, ref, send_sem.at[stream, phase, kind], recv_sem.at[stream, phase, kind],
            device(to["x"], to["y"], to["z"], core),
        )

    def streams(chunk):
        return range(3 * chunk, 3 * chunk + 3)

    def begin(chunk, phase):
        for s in streams(chunk):
            for kind in (2, 0, 1):
                move(s, phase, kind).start()

    def arrive(chunk, phase):
        for s in streams(chunk):
            for kind in range(3):
                move(s, phase, kind).wait_recv()

    def advance(chunk, phase):
        arrive(chunk, phase - 1)
        begin(chunk, phase)

    def sent(chunk, phases):
        for s in streams(chunk):
            for phase in phases:
                for kind in range(3):
                    move(s, phase, kind).wait_send()

    swaps = [
        remote(ids, ids_v, pair_send.at[0], pair_recv.at[0], sibling),
        remote(noise, noise2, pair_send.at[1], pair_recv.at[1], sibling),
        remote(vectors, vec.at[pl.ds(count, count)], pair_send.at[2], pair_recv.at[2], sibling),
    ]
    groups = []
    for i, target in enumerate([sibling] + across):
        for j, (source, place) in enumerate(tables):
            groups.append(remote(source, place, group_send.at[j, i], group_recv.at[j, i], target))

    begin(0, 0)
    for copy in swaps:
        copy.start()
    advance(0, 1)
    advance(0, 2)
    begin(1, 0)
    swaps[0].wait()
    ids_copy = pltpu.make_async_copy(ids_v, ids_s.at[1], local_sem.at[11])
    ids_copy.start()
    for copy in local:
        copy.wait()
    ids_copy.wait()
    sent(0, (0, 1))
    advance(1, 1)
    arrive(0, 2)
    begin(2, 0)
    begin(3, 0)

    def later(*steps):
        def run():
            for step in steps:
                step()
        return run

    def go(chunk, phase):
        return lambda: advance(chunk, phase)

    events = (
        {0: go(1, 2), 1: later(lambda: swaps[2].wait(), go(2, 1))},
        {0: go(2, 2), 1: later(*[copy.start for copy in groups], go(3, 1))},
        {0: go(3, 2)},
        {},
    )

    lane16 = lax.broadcasted_iota(jnp.int32, (16, 128), 1)
    masks = [(lane16 % 64) // 16 == r for r in range(4)]
    sign = jnp.where(lax.broadcasted_iota(jnp.int32, (64, 128), 1) < 64, -1.0, 1.0).astype(BF16)

    def times_i(block):
        return pltpu.roll(block, 64, 1) * sign

    keep = (lane16 % 16) == lax.broadcasted_iota(jnp.int32, (16, 128), 0)

    def compute(chunk, actions):
        ref = chunks[chunk]

        def step(turn, carry):
            for when, action in actions.items():
                pl.when(turn == when)(action)
            places = []
            part_of = lax.div(turn, count // STEP)
            for k in range(STEP):
                for j in range(2):
                    b = ids_s[part_of, j, lax.rem(turn, count // STEP) * STEP + k]
                    places.append((lax.rem(lax.div(b, 2), 2), lax.div(b, 4), lax.rem(b, 2) * 2))
            tees = []
            for xh in range(2):
                w = xh * 4 + chunk
                for k in range(STEP):
                    g = turn * STEP + k
                    rows = [
                        ref[xh * 2 + px, py, pl.ds(pz, 2)].reshape(64, 256)
                        for px, py, pz in places[2 * k : 2 * k + 2]
                    ]
                    tee = jnp.dot(
                        vec[g], jnp.concatenate(rows, 0), preferred_element_type=F32
                    ).astype(BF16)
                    diag[w, pl.ds(g, 1)] = diagonal(tee[:64, :128], masks, keep)
                    diag[8 + w, pl.ds(g, 1)] = diagonal(tee[64:, 128:], masks, keep)
                    tees.append(tee)
            for xh in range(2):
                w = xh * 4 + chunk
                left1, right1, left2, right2 = [], [], [], []
                for tee in tees[xh * STEP : (xh + 1) * STEP]:
                    a, b, c, d = tee[:64, :128], tee[:64, 128:], tee[64:, :128], tee[64:, 128:]
                    left1 += [a, d]
                    right1 += [a, times_i(a), d, times_i(d)]
                    left2.append(b)
                    right2 += [c, times_i(c)]
                for i, (left, right) in enumerate(((left1, right1), (left2, right2))):
                    acc[w, i] += jnp.dot(
                        jnp.concatenate(left, 1), jnp.concatenate(right, 0), preferred_element_type=F32
                    )
            return carry

        lax.fori_loop(0, 2 * count // STEP, step, 0)

    for chunk in range(4):
        if chunk:
            arrive(chunk, 2)
        compute(chunk, events[chunk])
    row16 = lax.broadcasted_iota(jnp.int32, (16, 128), 0)
    bias = jnp.zeros((16, 2 * count), F32)
    low16 = lane16 < 64
    for r in range(16):
        pick = row16 == jnp.where(low16, r % 8, 8 + r % 8)
        bias += lax.dot_general(
            pick.astype(BF16), diag[r].astype(BF16),
            (((1,), (1,)), ((), ())), preferred_element_type=F32,
        )
    bias = 2.0 * bias
    bias1[...] = bias
    eye = lax.broadcasted_iota(jnp.int32, (64, 128), 0) == (
        lax.broadcasted_iota(jnp.int32, (64, 128), 1) % 64
    )
    row8 = lax.broadcasted_iota(jnp.int32, (8, 128), 0)
    lane8 = lax.broadcasted_iota(jnp.int32, (8, 128), 1)
    lines = jnp.zeros((8, 128), F32)
    for w in range(8):
        square = acc[w, 0] + 2.0 * acc[w, 1]
        line = jnp.sum(jnp.where(eye, square, 0.0), axis=0, keepdims=True)
        lines = jnp.where(row8 == w, line, lines)
    kx = [jnp.where(lane8 < 64, lines, 0.0), jnp.where(lane8 < 64, 0.0, lines)]
    swaps[1].wait()

    def fields_of(ref):
        return jnp.concatenate(
            [jnp.where(core == 0, ref[0:4], ref[4:8]), jnp.where(core == 0, ref[8:12], ref[12:16])], 0
        )

    fields = jnp.concatenate([fields_of(noise1), fields_of(noise2)], 1)
    re, im = bias[:8], bias[8:]
    energy_re = 0.5 * (re * re - im * im) - kx[0]
    energy_im = re * im - kx[1]
    shift_re, shift_im = -ROOT * re, -ROOT * im
    phase_re = fields * shift_re - 0.5 * (shift_re * shift_re - shift_im * shift_im)
    phase_im = fields * shift_im - shift_re * shift_im
    lane_of = ((row8 // 4) * 2 + core) * 4 + row8 % 4
    result = jnp.zeros((8, 128), F32)
    for i, value in enumerate((energy_re, energy_im, phase_re, phase_im)):
        column_sum = jnp.sum(value, axis=1, keepdims=True)
        line = jnp.sum(jnp.where(lane8 == lane_of, column_sum, 0.0), axis=0, keepdims=True)
        result = jnp.where(row8 == i, line, result)
    def exchange(phase, targets, place, value):
        rounds[phase, place] = value
        part[phase] = value
        copies_out = [
            remote(part.at[phase], rounds.at[phase, place], send1.at[phase, i], recv1.at[phase, i], target)
            for i, target in enumerate(targets)
        ]
        for copy in copies_out:
            copy.start()
        return copies_out

    ring_x = [device((x + i) % 4, y, z, core) for i in (2, 1, 3)]
    ring_y = [device(x, (y + i) % 4, z, core) for i in (2, 1, 3)]
    round1 = exchange(0, ring_x, x, result)
    swap = remote(bias1, bias2, pair_send.at[3], pair_recv.at[3], sibling)
    swap.start()
    for copy in groups:
        copy.wait()
    scalars = [
        pltpu.make_async_copy(source, place, local_sem.at[12 + i])
        for i, (source, place) in enumerate(((w_all, w_s), (c_all, c_s), (o_all, o_s)))
    ]
    for copy in scalars:
        copy.start()
    for copy in scalars:
        copy.wait()
    lane1 = lax.broadcasted_iota(jnp.int32, (1, 128), 1)
    before = jnp.int32(0)
    sources = [jnp.int32(0)] * WG
    weight_line = jnp.zeros((1, 128), F32)
    for w in range(GROUPS * WG):
        live_copies = c_s[w // WG, 0, w % WG]
        weight_line = jnp.where(lane1 == w, w_s[w // WG, 0, w % WG], weight_line)
        for j in range(KMAX):
            hit = jnp.logical_and(j < live_copies, o_s[w // WG, w % WG, j] == grp)
            for s in range(WG):
                sources[s] = jnp.where(jnp.logical_and(hit, before == s), w, sources[s])
            before = before + jnp.where(hit, 1, 0)
    for s in range(WG):
        green_ref[s] = shards[sources[s]]

    for copy in round1:
        copy.wait()
    round2 = exchange(1, ring_y, y, jnp.sum(rounds[0, 0:4], axis=0))
    for copy in round2:
        copy.wait()
    round3 = exchange(2, column, core * 4 + z, jnp.sum(rounds[1, 0:4], axis=0))
    sent(0, (2,))
    for chunk in range(1, 4):
        sent(chunk, range(3))
    swap.wait()
    theirs = pltpu.roll(bias2[...], 64, 1)[:, :count]
    ours = bias[:, :count]
    for c in range(2):
        for xh in range(2):
            one = ours[c * 8 + xh * 4 : c * 8 + xh * 4 + 4]
            two = theirs[c * 8 + xh * 4 : c * 8 + xh * 4 + 4]
            force_ref[c, xh * 8 : xh * 8 + 8] = jnp.concatenate(
                [jnp.where(core == 0, one, two), jnp.where(core == 0, two, one)], 0
            )
    for copy in round3:
        copy.wait()
    total = jnp.sum(rounds[2], axis=0)
    new = weight_line * jnp.exp(total[2:3]) * jnp.maximum(jnp.cos(total[3:4]), 0.0)
    moved = jnp.zeros((1, 128), F32)
    for s in range(WG):
        picked = jnp.sum(jnp.where(lane1 == sources[s], new, 0.0), axis=1, keepdims=True)
        moved = jnp.where(lane1 == s, picked, moved)
    shifted = jnp.where(row8 == 2, new, total)
    turn_by = lax.rem(128 - grp * WG, 128)
    shifted = pltpu.roll(shifted, turn_by, 1)
    energy_ref[...] = shifted[0:2, :WG]
    new_ref[...] = shifted[2:3, :WG]
    moved_ref[...] = moved[:, :WG]


def fused(green, vectors, ids, noise, weights, copies, owners):
    vmem = pl.BlockSpec(memory_space=pltpu.VMEM)
    hbm = pl.BlockSpec(memory_space=pl.ANY)
    shape = jax.ShapeDtypeStruct
    count = vectors.shape[0]
    block = (green.shape[0], 2 * green.shape[3])
    dma = pltpu.SemaphoreType.DMA
    streams = len(STREAMS)
    I32 = jnp.int32
    return pl.pallas_call(
        fused_kernel,
        out_shape=(
            shape((2, GROUPS * WG, count), F32),
            shape((2, WG), F32),
            shape((1, WG), F32),
            shape((1, WG), F32),
            shape((WG,) + block, BF16),
        ),
        in_specs=[hbm] * 7,
        out_specs=(vmem,) * 5,
        scratch_shapes=[pltpu.VMEM((4, 4, 4) + block, BF16)] * 4
        + [
            pltpu.VMEM((2 * count,) + vectors.shape[1:], BF16),
            pltpu.VMEM(ids.shape, I32),
            pltpu.SMEM((2,) + ids.shape, I32),
            pltpu.VMEM(noise.shape, F32),
            pltpu.VMEM(noise.shape, F32),
            pltpu.VMEM((8, 2, 64, 128), F32),
            pltpu.VMEM((16, 2 * count, 128), F32),
            pltpu.VMEM((3, 8, 128), F32),
            pltpu.VMEM((3, 8, 8, 128), F32),
            pltpu.VMEM((16, 2 * count), F32),
            pltpu.VMEM((16, 2 * count), F32),
            pltpu.VMEM(green.shape, BF16),
            pltpu.VMEM((GROUPS * WG,) + block, BF16),
            pltpu.VMEM((GROUPS, 1, WG), F32),
            pltpu.VMEM((GROUPS, 1, WG), I32),
            pltpu.VMEM((GROUPS, WG, KMAX), I32),
            pltpu.SMEM((GROUPS, 1, WG), F32),
            pltpu.SMEM((GROUPS, 1, WG), I32),
            pltpu.SMEM((GROUPS, WG, KMAX), I32),
            dma((15,)), dma((streams, 3, 4)), dma((streams, 3, 4)),
            dma((4,)), dma((4,)), dma((4, 3)), dma((4, 3)),
            dma((3, 7)), dma((3, 7)),
        ],
        compiler_params=pltpu.CompilerParams(
            collective_id=0, has_side_effects=True, vmem_limit_bytes=63 * MB
        ),
        name="fused_step",
    )(green, vectors, ids, noise, weights, copies, owners)


def outputs_kernel(force, energy, new, moved, green, force_ref, energy_ref, new_ref, moved_ref, green_ref):
    force_ref[...] = force[...]
    energy_ref[...] = energy[...]
    new_ref[...] = new[...]
    moved_ref[...] = moved[...]
    wide = green[...].astype(F32)
    for c in range(2):
        part = jnp.concatenate([wide[:, :, h * 128 + c * 64 : h * 128 + c * 64 + 64] for h in range(2)], 2)
        green_ref[:, c] = jnp.swapaxes(part, 0, 1).astype(BF16)


def outputs(force, energy, new, moved, green):
    vmem = pl.BlockSpec(memory_space=pltpu.VMEM)
    slots, rows, columns = green.shape
    shape = jax.ShapeDtypeStruct
    return pl.pallas_call(
        outputs_kernel,
        out_shape=tuple(shape(a.shape, a.dtype) for a in (force, energy, new, moved))
        + (shape((rows, 2, slots, columns // 2), BF16),),
        in_specs=[vmem] * 5,
        out_specs=(vmem,) * 5,
        compiler_params=pltpu.CompilerParams(vmem_limit_bytes=63 * MB),
        name="outputs",
    )(force, energy, new, moved, green)


def body(green, chol_blocks, block_ids, noise, weights, copies, owners):
    force_bias, energy, new_weights, moved_weights, moved_green = outputs(*fused(
        green, chol_blocks, block_ids.T, noise, weights.reshape(1, WG), copies.reshape(1, WG), owners
    ))
    return (force_bias, energy, new_weights.reshape(WG), moved_green, moved_weights.reshape(WG))


def solution(mesh):
    return jax.shard_map(
        body,
        mesh=mesh,
        in_specs=(
            P("chol", None, "grp", None),
            P(("grp", "chol"), None, None),
            P(("grp", "chol"), None),
            P(None, ("grp", "chol")),
            P("grp"),
            P("grp"),
            P("grp", None),
        ),
        out_specs=(
            P(None, None, ("grp", "chol")),
            P(None, "grp"),
            P("grp"),
            P("chol", None, "grp", None),
            P("grp"),
        ),
        check_vma=False,
    )
```

```python
import functools
import math

import jax
import jax.numpy as jnp
from jax import lax
from jax.experimental import pallas as pl
from jax.experimental.pallas import tpu as pltpu
from jax.sharding import PartitionSpec as P

MESH = pl.DeviceIdType.MESH
BF16 = jnp.bfloat16
F32 = jnp.float32
KMAX = 4
GROUPS = 4
WG = 4
ROOT = math.sqrt(0.005)
MB = 2**20

def position():
    grp = lax.axis_index("grp")
    chol = lax.axis_index("chol")
    x = (grp // 2) * 2 + (chol // 4) % 2
    return x, chol // 8, chol % 4, grp % 2


def device(x, y, z, core):
    return ((x // 2) * 2 + core, y * 8 + (x % 2) * 4 + z)


WINDOWS = (((0, 16), (0, 256)), ((16, 16), (0, 128)), ((16, 16), (128, 128)))
ORDERS = ("xyz", "yzx", "zxy")
STREAMS = tuple(
    (chunk, *WINDOWS[i], ORDERS[(chunk + i) % 3]) for chunk in range(4) for i in range(3)
)
STEP = 64


def diagonal(block, masks, keep):
    merged = block[0:16]
    for r in range(1, 4):
        merged = jnp.where(masks[r], block[16 * r : 16 * r + 16], merged)
    return jnp.sum(jnp.where(keep, merged, jnp.zeros_like(merged)).astype(F32), axis=0, keepdims=True)


def fused_kernel(
    green, vectors, ids, noise, weights, copies, owners,
    force_ref, energy_ref, new_ref, moved_ref, green_ref,
    g0, g1, g2, g3, vec, ids_v, ids_s, noise1, noise2, acc, diag, part, rounds,
    bias1, bias2, green_v, shards, w_all, c_all, o_all, w_s, c_s, o_s,
    local_sem, send_sem, recv_sem, pair_send, pair_recv, group_send, group_recv,
    send1, recv1,
):
    chunks = (g0, g1, g2, g3)
    x, y, z, core = position()
    grp = lax.axis_index("grp")
    count = vectors.shape[0]
    here = {"x": x, "y": y, "z": z}
    sibling = device(x, y, z, 1 - core)
    across = [device((x + 2) % 4, y, z, core), device((x + 2) % 4, y, z, 1 - core)]
    column = [
        device(x, y, (z + i) % 4, (core + k) % 2)
        for k in range(2) for i in range(4) if i + k > 0
    ]
    everyone = column + [across[1]]
    everyone += [device((x + i) % 4, y, z, core) for i in (1, 2, 3)]
    everyone += [device(x, (y + i) % 4, z, core) for i in (1, 2, 3)]
    barrier = pltpu.get_barrier_semaphore()
    for target in everyone:
        pl.semaphore_signal(barrier, inc=1, device_id=target, device_id_type=MESH)

    load = pltpu.make_async_copy(green, green_v, local_sem.at[0])
    load.start()
    local = [
        pltpu.make_async_copy(vectors, vec.at[pl.ds(0, count)], local_sem.at[4]),
        pltpu.make_async_copy(ids, ids_s.at[0], local_sem.at[5]),
        pltpu.make_async_copy(noise, noise1, local_sem.at[6]),
    ]
    own_shards = shards.at[pl.ds(grp * WG, WG)]
    tables = [
        (own_shards, own_shards),
        (weights, w_all.at[grp]),
        (copies, c_all.at[grp]),
        (owners, o_all.at[grp]),
    ]
    local += [
        pltpu.make_async_copy(source, place, local_sem.at[7 + i]) for i, (source, place) in enumerate(tables) if i
    ]
    for copy in local:
        copy.start()
    acc[...] = jnp.zeros_like(acc)
    load.wait()
    parts = [jnp.swapaxes(green_v[:, c].astype(F32), 0, 1) for c in range(2)]
    for c in range(4):
        row = jnp.concatenate(
            [parts[i][c][:, h * 64 : h * 64 + 64] for h in range(2) for i in range(2)], 1
        ).astype(BF16)
        chunks[c][x, y, z] = row
        shards[grp * WG + c] = row
    pl.semaphore_wait(barrier, len(everyone))

    def remote(source, target, send, recv, where):
        return pltpu.make_async_remote_copy(
            src_ref=source, dst_ref=target, send_sem=send, recv_sem=recv,
            device_id=where, device_id_type=MESH,
        )

    def move(stream, phase, kind):
        chunk, rows, cols, order = STREAMS[stream]
        axis, free = order[phase], order[:phase]
        to = dict(here)
        to[axis] = (here[axis] + (1, 3, 2)[kind]) % 4
        index = [slice(None) if a in free else here[a] for a in "xyz"]
        ref = chunks[chunk].at[(*index, pl.ds(*rows), pl.ds(*cols))]
        return remote(
            ref, ref, send_sem.at[stream, phase, kind], recv_sem.at[stream, phase, kind],
            device(to["x"], to["y"], to["z"], core),
        )

    def streams(chunk):
        return range(3 * chunk, 3 * chunk + 3)

    def begin(chunk, phase):
        for s in streams(chunk):
            for kind in (2, 0, 1):
                move(s, phase, kind).start()

    def arrive(chunk, phase):
        for s in streams(chunk):
            for kind in range(3):
                move(s, phase, kind).wait_recv()

    def advance(chunk, phase):
        arrive(chunk, phase - 1)
        begin(chunk, phase)

    def sent(chunk, phases):
        for s in streams(chunk):
            for phase in phases:
                for kind in range(3):
                    move(s, phase, kind).wait_send()

    swaps = [
        remote(ids, ids_v, pair_send.at[0], pair_recv.at[0], sibling),
        remote(noise, noise2, pair_send.at[1], pair_recv.at[1], sibling),
        remote(vectors, vec.at[pl.ds(count, count)], pair_send.at[2], pair_recv.at[2], sibling),
    ]
    groups = []
    for i, target in enumerate([sibling] + across):
        for j, (source, place) in enumerate(tables):
            groups.append(remote(source, place, group_send.at[j, i], group_recv.at[j, i], target))

    begin(0, 0)
    for copy in swaps:
        copy.start()
    advance(0, 1)
    advance(0, 2)
    begin(1, 0)
    for copy in groups:
        copy.start()
    swaps[0].wait()
    ids_copy = pltpu.make_async_copy(ids_v, ids_s.at[1], local_sem.at[11])
    ids_copy.start()
    for copy in local:
        copy.wait()
    ids_copy.wait()
    sent(0, (0, 1))
    advance(1, 1)
    arrive(0, 2)
    begin(2, 0)
    begin(3, 0)

    def later(*steps):
        def run():
            for step in steps:
                step()
        return run

    def go(chunk, phase):
        return lambda: advance(chunk, phase)

    events = (
        {0: go(1, 2), 1: later(lambda: swaps[2].wait(), go(2, 1))},
        {0: go(2, 2), 1: go(3, 1)},
        {0: go(3, 2)},
        {},
    )

    lane16 = lax.broadcasted_iota(jnp.int32, (16, 128), 1)
    masks = [(lane16 % 64) // 16 == r for r in range(4)]
    sign = jnp.where(lax.broadcasted_iota(jnp.int32, (64, 128), 1) < 64, -1.0, 1.0).astype(BF16)

    def times_i(block):
        return pltpu.roll(block, 64, 1) * sign

    keep = (lane16 % 16) == lax.broadcasted_iota(jnp.int32, (16, 128), 0)

    def compute(chunk, actions):
        ref = chunks[chunk]

        def step(turn, carry):
            for when, action in actions.items():
                pl.when(turn == when)(action)
            places = []
            part_of = lax.div(turn, count // STEP)
            for k in range(STEP):
                for j in range(2):
                    b = ids_s[part_of, j, lax.rem(turn, count // STEP) * STEP + k]
                    places.append((lax.rem(lax.div(b, 2), 2), lax.div(b, 4), lax.rem(b, 2) * 2))
            tees = []
            for xh in range(2):
                w = xh * 4 + chunk
                for k in range(STEP):
                    g = turn * STEP + k
                    rows = [
                        ref[xh * 2 + px, py, pl.ds(pz, 2)].reshape(64, 256)
                        for px, py, pz in places[2 * k : 2 * k + 2]
                    ]
                    tee = jnp.dot(
                        vec[g], jnp.concatenate(rows, 0), preferred_element_type=F32
                    ).astype(BF16)
                    diag[w, pl.ds(g, 1)] = diagonal(tee[:64, :128], masks, keep)
                    diag[8 + w, pl.ds(g, 1)] = diagonal(tee[64:, 128:], masks, keep)
                    tees.append(tee)
            for xh in range(2):
                w = xh * 4 + chunk
                left1, right1, left2, right2 = [], [], [], []
                for tee in tees[xh * STEP : (xh + 1) * STEP]:
                    a, b, c, d = tee[:64, :128], tee[:64, 128:], tee[64:, :128], tee[64:, 128:]
                    left1 += [a, d]
                    right1 += [a, times_i(a), d, times_i(d)]
                    left2.append(b)
                    right2 += [c, times_i(c)]
                for i, (left, right) in enumerate(((left1, right1), (left2, right2))):
                    acc[w, i] += jnp.dot(
                        jnp.concatenate(left, 1), jnp.concatenate(right, 0), preferred_element_type=F32
                    )
            return carry

        lax.fori_loop(0, 2 * count // STEP, step, 0)

    for chunk in range(4):
        if chunk:
            arrive(chunk, 2)
        compute(chunk, events[chunk])
    row16 = lax.broadcasted_iota(jnp.int32, (16, 128), 0)
    bias = jnp.zeros((16, 2 * count), F32)
    low16 = lane16 < 64
    for r in range(16):
        pick = row16 == jnp.where(low16, r % 8, 8 + r % 8)
        bias += lax.dot_general(
            pick.astype(BF16), diag[r].astype(BF16),
            (((1,), (1,)), ((), ())), preferred_element_type=F32,
        )
    bias = 2.0 * bias
    bias1[...] = bias
    eye = lax.broadcasted_iota(jnp.int32, (64, 128), 0) == (
        lax.broadcasted_iota(jnp.int32, (64, 128), 1) % 64
    )
    row8 = lax.broadcasted_iota(jnp.int32, (8, 128), 0)
    lane8 = lax.broadcasted_iota(jnp.int32, (8, 128), 1)
    lines = jnp.zeros((8, 128), F32)
    for w in range(8):
        square = acc[w, 0] + 2.0 * acc[w, 1]
        line = jnp.sum(jnp.where(eye, square, 0.0), axis=0, keepdims=True)
        lines = jnp.where(row8 == w, line, lines)
    kx = [jnp.where(lane8 < 64, lines, 0.0), jnp.where(lane8 < 64, 0.0, lines)]
    swaps[1].wait()

    def fields_of(ref):
        return jnp.concatenate(
            [jnp.where(core == 0, ref[0:4], ref[4:8]), jnp.where(core == 0, ref[8:12], ref[12:16])], 0
        )

    fields = jnp.concatenate([fields_of(noise1), fields_of(noise2)], 1)
    re, im = bias[:8], bias[8:]
    energy_re = 0.5 * (re * re - im * im) - kx[0]
    energy_im = re * im - kx[1]
    shift_re, shift_im = -ROOT * re, -ROOT * im
    phase_re = fields * shift_re - 0.5 * (shift_re * shift_re - shift_im * shift_im)
    phase_im = fields * shift_im - shift_re * shift_im
    lane_of = ((row8 // 4) * 2 + core) * 4 + row8 % 4
    result = jnp.zeros((8, 128), F32)
    for i, value in enumerate((energy_re, energy_im, phase_re, phase_im)):
        column_sum = jnp.sum(value, axis=1, keepdims=True)
        line = jnp.sum(jnp.where(lane8 == lane_of, column_sum, 0.0), axis=0, keepdims=True)
        result = jnp.where(row8 == i, line, result)
    def exchange(phase, targets, place, value):
        rounds[phase, place] = value
        part[phase] = value
        copies_out = [
            remote(part.at[phase], rounds.at[phase, place], send1.at[phase, i], recv1.at[phase, i], target)
            for i, target in enumerate(targets)
        ]
        for copy in copies_out:
            copy.start()
        return copies_out

    ring_x = [device((x + i) % 4, y, z, core) for i in (2, 1, 3)]
    ring_y = [device(x, (y + i) % 4, z, core) for i in (2, 1, 3)]
    round1 = exchange(0, ring_x, x, result)
    swap = remote(bias1, bias2, pair_send.at[3], pair_recv.at[3], sibling)
    swap.start()
    for copy in groups:
        copy.wait()
    scalars = [
        pltpu.make_async_copy(source, place, local_sem.at[12 + i])
        for i, (source, place) in enumerate(((w_all, w_s), (c_all, c_s), (o_all, o_s)))
    ]
    for copy in scalars:
        copy.start()
    for copy in scalars:
        copy.wait()
    lane1 = lax.broadcasted_iota(jnp.int32, (1, 128), 1)
    before = jnp.int32(0)
    sources = [jnp.int32(0)] * WG
    weight_line = jnp.zeros((1, 128), F32)
    for w in range(GROUPS * WG):
        live_copies = c_s[w // WG, 0, w % WG]
        weight_line = jnp.where(lane1 == w, w_s[w // WG, 0, w % WG], weight_line)
        for j in range(KMAX):
            hit = jnp.logical_and(j < live_copies, o_s[w // WG, w % WG, j] == grp)
            for s in range(WG):
                sources[s] = jnp.where(jnp.logical_and(hit, before == s), w, sources[s])
            before = before + jnp.where(hit, 1, 0)
    for s in range(WG):
        green_ref[s] = shards[sources[s]]

    for copy in round1:
        copy.wait()
    round2 = exchange(1, ring_y, y, jnp.sum(rounds[0, 0:4], axis=0))
    for copy in round2:
        copy.wait()
    round3 = exchange(2, column, core * 4 + z, jnp.sum(rounds[1, 0:4], axis=0))
    sent(0, (2,))
    for chunk in range(1, 4):
        sent(chunk, range(3))
    swap.wait()
    theirs = pltpu.roll(bias2[...], 64, 1)[:, :count]
    ours = bias[:, :count]
    for c in range(2):
        for xh in range(2):
            one = ours[c * 8 + xh * 4 : c * 8 + xh * 4 + 4]
            two = theirs[c * 8 + xh * 4 : c * 8 + xh * 4 + 4]
            force_ref[c, xh * 8 : xh * 8 + 8] = jnp.concatenate(
                [jnp.where(core == 0, one, two), jnp.where(core == 0, two, one)], 0
            )
    for copy in round3:
        copy.wait()
    total = jnp.sum(rounds[2], axis=0)
    new = weight_line * jnp.exp(total[2:3]) * jnp.maximum(jnp.cos(total[3:4]), 0.0)
    moved = jnp.zeros((1, 128), F32)
    for s in range(WG):
        picked = jnp.sum(jnp.where(lane1 == sources[s], new, 0.0), axis=1, keepdims=True)
        moved = jnp.where(lane1 == s, picked, moved)
    shifted = jnp.where(row8 == 2, new, total)
    turn_by = lax.rem(128 - grp * WG, 128)
    shifted = pltpu.roll(shifted, turn_by, 1)
    energy_ref[...] = shifted[0:2, :WG]
    new_ref[...] = shifted[2:3, :WG]
    moved_ref[...] = moved[:, :WG]


def fused(green, vectors, ids, noise, weights, copies, owners):
    vmem = pl.BlockSpec(memory_space=pltpu.VMEM)
    hbm = pl.BlockSpec(memory_space=pl.ANY)
    shape = jax.ShapeDtypeStruct
    count = vectors.shape[0]
    block = (green.shape[0], 2 * green.shape[3])
    dma = pltpu.SemaphoreType.DMA
    streams = len(STREAMS)
    I32 = jnp.int32
    return pl.pallas_call(
        fused_kernel,
        out_shape=(
            shape((2, GROUPS * WG, count), F32),
            shape((2, WG), F32),
            shape((1, WG), F32),
            shape((1, WG), F32),
            shape((WG,) + block, BF16),
        ),
        in_specs=[hbm] * 7,
        out_specs=(vmem,) * 5,
        scratch_shapes=[pltpu.VMEM((4, 4, 4) + block, BF16)] * 4
        + [
            pltpu.VMEM((2 * count,) + vectors.shape[1:], BF16),
            pltpu.VMEM(ids.shape, I32),
            pltpu.SMEM((2,) + ids.shape, I32),
            pltpu.VMEM(noise.shape, F32),
            pltpu.VMEM(noise.shape, F32),
            pltpu.VMEM((8, 2, 64, 128), F32),
            pltpu.VMEM((16, 2 * count, 128), F32),
            pltpu.VMEM((3, 8, 128), F32),
            pltpu.VMEM((3, 8, 8, 128), F32),
            pltpu.VMEM((16, 2 * count), F32),
            pltpu.VMEM((16, 2 * count), F32),
            pltpu.VMEM(green.shape, BF16),
            pltpu.VMEM((GROUPS * WG,) + block, BF16),
            pltpu.VMEM((GROUPS, 1, WG), F32),
            pltpu.VMEM((GROUPS, 1, WG), I32),
            pltpu.VMEM((GROUPS, WG, KMAX), I32),
            pltpu.SMEM((GROUPS, 1, WG), F32),
            pltpu.SMEM((GROUPS, 1, WG), I32),
            pltpu.SMEM((GROUPS, WG, KMAX), I32),
            dma((15,)), dma((streams, 3, 4)), dma((streams, 3, 4)),
            dma((4,)), dma((4,)), dma((4, 3)), dma((4, 3)),
            dma((3, 7)), dma((3, 7)),
        ],
        compiler_params=pltpu.CompilerParams(
            collective_id=0, has_side_effects=True, vmem_limit_bytes=63 * MB
        ),
        name="fused_step",
    )(green, vectors, ids, noise, weights, copies, owners)


def outputs_kernel(force, energy, new, moved, green, force_ref, energy_ref, new_ref, moved_ref, green_ref):
    force_ref[...] = force[...]
    energy_ref[...] = energy[...]
    new_ref[...] = new[...]
    moved_ref[...] = moved[...]
    wide = green[...].astype(F32)
    for c in range(2):
        part = jnp.concatenate([wide[:, :, h * 128 + c * 64 : h * 128 + c * 64 + 64] for h in range(2)], 2)
        green_ref[:, c] = jnp.swapaxes(part, 0, 1).astype(BF16)


def outputs(force, energy, new, moved, green):
    vmem = pl.BlockSpec(memory_space=pltpu.VMEM)
    slots, rows, columns = green.shape
    shape = jax.ShapeDtypeStruct
    return pl.pallas_call(
        outputs_kernel,
        out_shape=tuple(shape(a.shape, a.dtype) for a in (force, energy, new, moved))
        + (shape((rows, 2, slots, columns // 2), BF16),),
        in_specs=[vmem] * 5,
        out_specs=(vmem,) * 5,
        compiler_params=pltpu.CompilerParams(vmem_limit_bytes=63 * MB),
        name="outputs",
    )(force, energy, new, moved, green)


def body(green, chol_blocks, block_ids, noise, weights, copies, owners):
    force_bias, energy, new_weights, moved_weights, moved_green = outputs(*fused(
        green, chol_blocks, block_ids.T, noise, weights.reshape(1, WG), copies.reshape(1, WG), owners
    ))
    return (force_bias, energy, new_weights.reshape(WG), moved_green, moved_weights.reshape(WG))


def solution(mesh):
    return jax.shard_map(
        body,
        mesh=mesh,
        in_specs=(
            P("chol", None, "grp", None),
            P(("grp", "chol"), None, None),
            P(("grp", "chol"), None),
            P(None, ("grp", "chol")),
            P("grp"),
            P("grp"),
            P("grp", None),
        ),
        out_specs=(
            P(None, None, ("grp", "chol")),
            P(None, "grp"),
            P("grp"),
            P("chol", None, "grp", None),
            P("grp"),
        ),
        check_vma=False,
    )
```
